512 devices in a mesh: section: 16 (over x_hi, y), expert: 8 (over z), dp: 4 (over x_lo, core).
Axes of the slice: x: 4 (x_hi: 2, x_lo: 2; x = x_hi * 2 + x_lo), y: 8, z: 8, core: 2. Of those that a mesh axis runs over, the one named last changes fastest.
Arguments:
- tokens: bfloat16 [2048, 6144], P('section', ('dp', 'expert')), may hold values from -6 to 6
- norm_gain: float32 [6144], P(('dp', 'expert')), may hold values from 0.25 to 1.75
- routes: int32 [2048, 2], P('section'), may hold values from 0 to 7, all different within a row; in each aligned block of 128 rows (0 to 127, 128 to 255, ...) at most 48 rows name the same one
- gates: float32 [2048, 2], P('section'), may hold values from 0.1 to 1
- w_gate: bfloat16 [8, 6144, 8192], P('expert', 'dp', 'section'), may hold values from -0.078125 to 0.078125
- w_up: bfloat16 [8, 6144, 8192], P('expert', 'dp', 'section'), may hold values from -0.078125 to 0.078125
- w_down: bfloat16 [8, 8192, 6144], P('expert', 'section', 'dp'), may hold values from -0.0625 to 0.0625
Outputs:
- mixed: bfloat16 [2048, 6144], P('section', ('dp', 'expert'))
The draws below stay inside these ranges and needn't reach their ends.
Inputs may be any that keep to these rules, and one draw needn't show every extreme that they name: `routes`: each token names two different experts. Within each aligned block of 128 rows no expert is named by more than 48 rows, and in some block one expert is named by exactly 48.
All inputs are finite; a program needn't handle non-finite values.
Results may differ from the reference program's by a relative error of at most 0.015.
Values may be sent and summed in bfloat16 or wider, within the bound.
A program may use at most 64 MiB of HBM per device.

```python
import math
import jax
import jax.numpy as jnp
import numpy as np
from jax import lax

D = 6144
FF = 8192
TOK_DEV = 128
EXPERTS = 8
CAP = 48
TOKENS = 2048
N_SECTION = 16
N_DP = 4


def block_scale(rng, dims, pieces, least, largest):
    def one(dim, blocks):
        heights = jax.random.uniform(jax.random.fold_in(jax.random.fold_in(rng, 6), dim), (blocks,), jnp.float32, least / len(pieces), largest / len(pieces))
        return jnp.repeat(jnp.exp(heights), dims[dim] // blocks).reshape((-1,) + (1,) * (len(dims) - dim - 1))

    factor_of = one(*pieces[0])
    for cut in pieces[1:]:
        factor_of = factor_of * one(*cut)
    return factor_of


def deal_out(rng, own, number, rows, amount, top, most, skew):
    ranking = jax.random.permutation(rng, amount)
    crowded, usual = shares(amount, rows * top, most, skew, True), shares(amount, rows * top, most, skew, False)
    places = jnp.arange(amount)

    def named(sizes, rotation):
        used = int((sizes > 0).sum())
        fixed = max(1, used // 4)
        moved = fixed + (places - fixed + rotation * (used - fixed)) % max(1, amount - fixed)
        return jnp.zeros((amount,), jnp.int32).at[ranking[jnp.where(places < fixed, places, moved)]].set(jnp.asarray(sizes, jnp.int32))

    sizes = jnp.where(number % 4 == 0, named(crowded, number // 4), named(usual, number - number // 4 - 1))
    mixed = jax.random.permutation(jax.random.fold_in(own, 3), amount)
    donor, receiver = mixed[0:amount // 2 * 2:2], mixed[1:amount // 2 * 2:2]
    slack = jnp.minimum(sizes[donor] - 1, most - sizes[receiver]) // 2
    slack = jnp.where((donor == ranking[0]) | (receiver == ranking[0]) | (sizes[receiver] == 0), 0, jnp.maximum(slack, 0))
    moved = jax.random.randint(jax.random.fold_in(own, 4), (amount // 2,), 0, 1 << 20) % (slack + 1)
    sizes = sizes.at[donor].add(-moved).at[receiver].add(moved)
    items = jnp.searchsorted(jnp.cumsum(sizes), jnp.arange(rows * top), side="right").astype(jnp.int32)
    table = items.reshape(top, rows).T
    table = table[jax.random.permutation(jax.random.fold_in(own, 1), rows)]
    rotation = jax.random.randint(jax.random.fold_in(own, 2), (rows, 1), 0, top)
    return jnp.take_along_axis(table, (jnp.arange(top)[None, :] + rotation) % top, axis=1)


def shares(amount, total, reach, skew, full):
    portions = [(1 << 20) // math.isqrt(standing ** skew) + 1 for standing in range(1, amount + 1)]
    largest = reach if full else min(reach, max(-(-total // amount), total * portions[0] // sum(portions)))
    least = 1 if total - largest >= amount - 1 else 0
    holding, rest = [largest] + [least] * (amount - 1), total - largest - least * (amount - 1)
    while rest > 0:
        movable = [i for i in range(1, amount) if holding[i] < largest] or [i for i in range(1, amount) if holding[i] < reach]
        pool, remaining = sum([portions[i] for i in movable]), rest
        for i in movable:
            extra = min(reach - holding[i], max(1, remaining * portions[i] // pool), rest)
            holding[i] = holding[i] + extra
            rest = rest - extra
    return np.array(holding)


def scatter_about(stream_key, dims, scale, most, cuts=(), kind=jnp.bfloat16):
    gain = block_scale(stream_key, dims, cuts, -0.22, 0.18) if cuts else 1.0
    array = jax.random.normal(stream_key, dims, jnp.float32) * scale * gain
    return jnp.minimum(jnp.maximum(array, -most), most).astype(kind)


def setup_inputs(seed: int = 0) -> dict:
    keys = jax.random.split(jax.random.key(seed), 8)
    tokens = scatter_about(keys[0], (TOKENS, D), 1.0, 6.0, ((0, 16), (1, 32)))
    norm_gain = jnp.clip(1.0 + 0.15 * jax.random.normal(keys[1], (D,), jnp.float32), 0.25, 1.75)
    routes_keys = jax.random.split(jax.random.fold_in(keys[2], 1), TOKENS // TOK_DEV)
    routes_turns = jax.random.permutation(jax.random.fold_in(keys[2], 3), TOKENS // TOK_DEV)
    routes = jax.vmap(lambda own, number: deal_out(jax.random.fold_in(keys[2], 2), own, number, TOK_DEV, EXPERTS, 2, CAP, 2))(routes_keys, routes_turns).reshape((TOKENS, 2))
    gates = jnp.clip(jnp.exp(math.log(1.0) - 2.3025851 * jax.random.uniform(keys[3], (TOKENS, 2), jnp.float32) ** block_scale(keys[3], (TOKENS, 2), ((0, 16),), -0.2, 0.2)), 0.1, 1.0)
    w_gate = scatter_about(keys[4], (EXPERTS, D, FF), D ** -0.5, 0.078125, ((0, 8), (1, 4), (2, 16)))
    w_up = scatter_about(keys[5], (EXPERTS, D, FF), D ** -0.5, 0.078125, ((0, 8), (1, 4), (2, 16)))
    w_down = scatter_about(keys[6], (EXPERTS, FF, D), FF ** -0.5, 0.0625, ((0, 8), (1, 16), (2, 4)))
    return {"tokens": tokens, "norm_gain": norm_gain, "routes": routes, "gates": gates, "w_gate": w_gate, "w_up": w_up, "w_down": w_down}


def reference(tokens, norm_gain, routes, gates, w_gate, w_up, w_down):
    stream = tokens.astype(jnp.float32)
    scale = lax.rsqrt(lax.optimization_barrier(jnp.mean(stream * stream, axis=-1, keepdims=True)) + 1e-05)
    normed = (stream * scale * norm_gain[None, :]).astype(jnp.bfloat16)
    padded = jnp.concatenate([normed, jnp.zeros((1, D), jnp.bfloat16)], 0)
    totals = jnp.concatenate([stream, jnp.zeros((1, D), jnp.float32)], 0)
    limit = min(TOKENS, N_SECTION * CAP)
    width = D // N_DP
    slice_units = FF // N_SECTION

    def add_expert(expert, totals):
        matched = routes == expert
        weight = lax.optimization_barrier(jnp.sum(jnp.where(matched, gates, jnp.zeros_like(gates)), axis=-1))
        weight = jnp.concatenate([weight, jnp.zeros((1,), weight.dtype)], 0)
        named = jnp.any(matched, axis=-1)
        rows_at = jnp.nonzero(named, size=limit, fill_value=TOKENS)[0].astype(jnp.int32)
        rows = padded[rows_at]
        gate_all = w_gate[expert]
        up_all = w_up[expert]
        down_all = w_down[expert]

        def width_slice(index, carry):
            gate_sum, up_sum = carry
            start = jnp.asarray(index * width).astype(jnp.int32)
            part_rows = lax.dynamic_slice_in_dim(rows, start, width, 1)
            gate_rows = lax.dynamic_slice_in_dim(gate_all, start, width, 0)
            up_rows = lax.dynamic_slice_in_dim(up_all, start, width, 0)
            gate_part = lax.optimization_barrier(jnp.dot(part_rows, gate_rows, preferred_element_type=jnp.float32).astype(jnp.bfloat16))
            up_part = lax.optimization_barrier(jnp.dot(part_rows, up_rows, preferred_element_type=jnp.float32).astype(jnp.bfloat16))
            return (gate_sum + gate_part.astype(jnp.float32), up_sum + up_part.astype(jnp.float32))
        empty = jnp.zeros((limit, FF), jnp.float32)
        gate_pre, up_pre = lax.fori_loop(0, N_DP, width_slice, (empty, empty))
        hidden = (jax.nn.silu(gate_pre) * up_pre).astype(jnp.bfloat16)

        def unit_slice(index, total):
            start = jnp.asarray(index * slice_units).astype(jnp.int32)
            part_hidden = lax.dynamic_slice_in_dim(hidden, start, slice_units, 1)
            part_down = lax.dynamic_slice_in_dim(down_all, start, slice_units, 0)
            down_part = lax.optimization_barrier(jnp.dot(part_hidden, part_down, preferred_element_type=jnp.float32).astype(jnp.bfloat16))
            return total + down_part.astype(jnp.float32)
        expert_out = lax.fori_loop(0, N_SECTION, unit_slice, jnp.zeros((limit, D), jnp.float32)).astype(jnp.bfloat16)
        return totals.at[rows_at].add(weight[rows_at][:, None] * expert_out.astype(jnp.float32))
    totals = lax.fori_loop(0, EXPERTS, add_expert, totals)
    return totals[:TOKENS].astype(jnp.bfloat16)
```

```python
import functools

import jax
import jax.numpy as jnp
from jax import lax
from jax.experimental import pallas as pl
from jax.experimental.pallas import tpu as pltpu
from jax.sharding import PartitionSpec as P

D = 6144
EPS = 1e-05
N_X = 2
F32 = jnp.float32
BF16 = jnp.bfloat16
LANES = 128


def dot(a, b):
    return jnp.dot(a, b, preferred_element_type=F32)


def dot_last(a, b):
    return lax.dot_general(a, b, (((1,), (1,)), ((), ())), preferred_element_type=F32)


def dot_first(a, b):
    return lax.dot_general(a, b, (((0,), (0,)), ((), ())), preferred_element_type=F32)


def split3(v):
    high = v.astype(BF16).astype(F32)
    rest = v - high
    mid = rest.astype(BF16).astype(F32)
    return high, mid, rest - mid


def pack(rows):
    cap = rows.shape[0]
    half = cap // 2
    tail = rows[:, LANES:]
    below = jnp.concatenate([tail[:half], tail[half:]], axis=1)
    pad = -half % 16
    if pad:
        below = jnp.concatenate([below, jnp.zeros((pad, LANES), F32)], axis=0)
    return rows[:, :LANES], below


def kernel(
    sizes,
    tok_ref,
    gain_ref,
    routes_ref,
    gates_ref,
    wg_hbm,
    wu_hbm,
    wd_hbm,
    out_ref,
    wg,
    wu,
    wd,
    w_sem,
    mix_top,
    mix_low,
    go,
    got,
    ss_out,
    ss_in,
    ag,
    part_out,
    part_in,
    hid,
    rs_out,
    rs_in,
    own,
    xr_out,
    xr_in,
    bk_out,
    bk_in,
    go_s,
    go_r,
    ss_s,
    ss_r,
    x_s,
    x_r,
    ag_s,
    ag_r,
    part_s,
    part_r,
    hid_s,
    hid_r,
    rs_s,
    rs_r,
    xr_s,
    xr_r,
    bk_s,
    bk_r,
):
    n_y, n_e, n_d, cap = sizes
    half = cap // 2
    low = half + (-half % 16)
    n_tok = tok_ref.shape[1]
    n_feat = tok_ref.shape[0]
    width = n_feat * n_e
    rows = N_X * cap
    sec = lax.axis_index("section")
    z = lax.axis_index("expert")
    d = lax.axis_index("dp")
    xh = lax.div(sec, n_y)
    y = lax.rem(sec, n_y)
    up = xh * n_y + lax.rem(y + 1, n_y)
    down = xh * n_y + lax.rem(y + n_y - 1, n_y)
    across = (1 - xh) * n_y + y

    def ring(h):
        return xh * n_y + lax.rem(y + 1 + h * (n_y - 2), n_y)

    def remote(src, dst, send, recv, **where):
        return pltpu.make_async_remote_copy(
            src_ref=src,
            dst_ref=dst,
            send_sem=send,
            recv_sem=recv,
            device_id=where,
            device_id_type=pl.DeviceIdType.MESH,
        )

    loads = [
        pltpu.make_async_copy(src.at[0], dst, w_sem.at[i])
        for i, (src, dst) in enumerate(((wg_hbm, wg), (wu_hbm, wu), (wd_hbm, wd)))
    ]
    for load in loads:
        load.start()

    barrier = pltpu.get_barrier_semaphore()
    for i in range(1, n_e):
        pl.semaphore_signal(barrier, inc=1, device_id={"expert": lax.rem(z + i, n_e)}, device_id_type=pl.DeviceIdType.MESH)
    for i in range(1, n_d):
        pl.semaphore_signal(barrier, inc=1, device_id={"dp": lax.rem(d + i, n_d)}, device_id_type=pl.DeviceIdType.MESH)
    for to in (up, down, across):
        pl.semaphore_signal(barrier, inc=1, device_id={"section": to}, device_id_type=pl.DeviceIdType.MESH)

    first = routes_ref[0:1, :]
    second = routes_ref[1:2, :]
    expert_ids = lax.broadcasted_iota(jnp.int32, (n_e, n_tok), 0)
    named = (first == expert_ids) | (second == expert_ids)
    earlier = (
        lax.broadcasted_iota(jnp.int32, (n_tok, n_tok), 0) < lax.broadcasted_iota(jnp.int32, (n_tok, n_tok), 1)
    )
    count = dot(jnp.where(named, 1.0, 0.0).astype(BF16), jnp.where(earlier, 1.0, 0.0).astype(BF16))
    slot = jnp.where(named, count, -1.0)
    weight = jnp.where(first == expert_ids, gates_ref[0:1, :], gates_ref[1:2, :])
    number = lax.broadcasted_iota(jnp.int32, (cap, n_tok), 0).astype(F32)
    low_row = lax.broadcasted_iota(jnp.int32, (low, n_tok), 0)
    low_number = jnp.where(low_row < half, low_row, 4 * cap).astype(F32)
    tops, lows, lows_more = [], [], []
    for e in range(n_e):
        mine = slot[e : e + 1, :]
        w = weight[e : e + 1, :]
        top = jnp.where(mine == number, 1.0, 0.0)
        low_a = jnp.where(mine == low_number, 1.0, 0.0)
        low_b = jnp.where(mine == low_number + half, 1.0, 0.0)
        tops.append(top.astype(BF16))
        lows.append(low_a.astype(BF16))
        lows_more.append(low_b.astype(BF16))
        for at, (part, store, size) in enumerate(((top, mix_top, cap), (low_a, mix_low, low), (low_b, mix_low, low))):
            lead = 0 if at == 0 else 2 * (at - 1)
            value = part * w
            high = value.astype(BF16)
            store[lead, e * size : (e + 1) * size, :] = high
            store[lead + 1, e * size : (e + 1) * size, :] = (value - high.astype(F32)).astype(BF16)
    tok = tok_ref[...]
    tail = tok[LANES:]
    blank = jnp.zeros_like(tail)
    sent_top = dot_last(jnp.concatenate(tops, axis=0), tok[:LANES])
    sent_low = dot_last(jnp.concatenate(lows, axis=0), jnp.concatenate([tail, blank], axis=0)) + dot_last(
        jnp.concatenate(lows_more, axis=0), jnp.concatenate([blank, tail], axis=0)
    )
    gain = gain_ref[...]
    gain_rows = list(split3(gain[:, :LANES])) + [
        jnp.concatenate([v, jnp.zeros((1, 2 * LANES - n_feat), F32)], axis=1) for v in split3(gain[:, LANES:])
    ]
    gain_block = jnp.concatenate(gain_rows + [jnp.zeros((2, LANES), F32)], axis=0)
    go[:, 0:cap, :] = sent_top.astype(BF16).reshape(n_e, cap, LANES)
    for e in range(n_e):
        block = sent_low[e * low : (e + 1) * low]
        go[e, cap : cap + low, :] = jnp.concatenate([block[:half], gain_block], axis=0).astype(BF16)

    pl.semaphore_wait(barrier, n_e - 1 + n_d - 1 + 3)

    def z_copy(src, dst, send, recv, i, outgoing):
        to = lax.rem(z + i, n_e)
        at = z if outgoing else to
        return remote(src.at[to], dst.at[at], send.at[i - 1], recv.at[at], expert=to)

    order = sorted(range(1, n_e), key=lambda i: -min(i, n_e - i))
    for i in order:
        z_copy(go, got, go_s, go_r, i, True).start()
    got[z] = go[z]
    for i in order[::-1]:
        z_copy(go, got, go_s, go_r, i, False).wait_recv()

    pieces, gains = [], []
    for e in range(n_e):
        block = got[e].astype(F32)
        below = block[cap : cap + half]
        edge = n_feat - LANES
        pieces.append(
            jnp.concatenate(
                [block[:cap], jnp.concatenate([below[:, :edge], below[:, edge : 2 * edge]], axis=0)], axis=1
            )
        )
        g = block[cap + half : cap + half + 8]
        gains.append(g[0:1] + g[1:2] + g[2:3])
        gains.append((g[3:4] + g[4:5] + g[5:6])[:, :edge])
    arrived = jnp.concatenate(pieces, axis=1)
    gain_all = jnp.concatenate(gains, axis=1)
    squares = jnp.sum(arrived * arrived, axis=1, keepdims=True)
    eye = lax.broadcasted_iota(jnp.int32, (cap, LANES), 0) == lax.broadcasted_iota(jnp.int32, (cap, LANES), 1)
    ss_out[...] = jnp.broadcast_to(jnp.sum(jnp.where(eye, squares, 0.0), axis=0, keepdims=True), ss_out.shape)

    def d_copy(src, dst, send, recv, i, outgoing):
        to = lax.rem(d + i, n_d)
        at = d if outgoing else to
        return remote(src, dst.at[at], send.at[i - 1], recv.at[at], dp=to)

    for i in range(1, n_d):
        d_copy(ss_out, ss_in, ss_s, ss_r, i, True).start()
    for i in range(1, n_d):
        d_copy(ss_out, ss_in, ss_s, ss_r, i, False).wait_recv()
    total = ss_out[0:1, :]
    for i in range(1, n_d):
        total = total + ss_in[lax.rem(d + i, n_d)][0:1, :]
    sums = jnp.sum(jnp.where(eye, total, 0.0), axis=1, keepdims=True)
    scale = lax.rsqrt(sums / (n_d * width) + EPS)
    ag[0, xh] = (arrived * scale * gain_all).astype(BF16)

    def ag_copy(b, h):
        return remote(ag.at[b, h], ag.at[b + 1, h], ag_s.at[b, h], ag_r.at[b + 1, h], section=ring(h))

    def ag_wait(b, h):
        remote(ag.at[b, h], ag.at[b, h], ag_s.at[b, h], ag_r.at[b, h], section=ring(h)).wait_recv()

    x_copy = remote(ag.at[0, xh], ag.at[0, xh], x_s, x_r, section=across)
    x_copy.start()
    ag_copy(0, xh).start()
    remote(ag.at[0, 1 - xh], ag.at[0, 1 - xh], x_s, x_r, section=across).wait_recv()
    ag_copy(0, 1 - xh).start()
    for load in loads:
        load.wait()

    def part_copy(b, i, outgoing):
        to = lax.rem(d + i, n_d)
        if outgoing:
            return remote(part_out.at[b, to], part_in.at[b, d], part_s.at[b, i - 1], part_r.at[b, d], dp=to)
        return remote(part_out.at[b, to], part_in.at[b, to], part_s.at[b, i - 1], part_r.at[b, to], dp=to)

    def hid_copy(b, i, outgoing):
        to = lax.rem(d + i, n_d)
        at = d if outgoing else to
        return remote(hid.at[b, d], hid.at[b, at], hid_s.at[b, i - 1], hid_r.at[b, at], dp=to)

    def rs_copy(b, h):
        return remote(rs_out.at[b, h], rs_in.at[b + 1, h], rs_s.at[b, h], rs_r.at[b + 1, h], section=ring(h))

    def rs_wait(b, h):
        remote(rs_in.at[b, h], rs_in.at[b, h], rs_s.at[0, h], rs_r.at[b, h], section=ring(h)).wait_recv()

    unit = wg.shape[1] // n_d

    def tick(t, carry):
        @pl.when(t < n_y)
        def _():
            @pl.when(t > 0)
            def _():
                for h in range(N_X):
                    ag_wait(t, h)

                    @pl.when(t < n_y - 1)
                    def _():
                        ag_copy(t, h).start()

            block = ag[t].reshape(rows, width)
            gate = dot(block, wg[...]).astype(BF16)
            upper = dot(block, wu[...]).astype(BF16)
            for p in range(n_d):
                part_out[t, p, :, 0:unit] = gate[:, p * unit : (p + 1) * unit]
                part_out[t, p, :, unit : 2 * unit] = upper[:, p * unit : (p + 1) * unit]
            for i in range(1, n_d):
                part_copy(t, i, True).start()

        @pl.when((t > 0) & (t < n_y + 1))
        def _():
            b = t - 1
            both = part_out[b, d].astype(F32)
            for i in range(1, n_d):
                part_copy(b, i, False).wait_recv()
                both = both + part_in[b, lax.rem(d + i, n_d)].astype(F32)
            g = both[:, 0:unit]
            hid[b, d] = (g / (1.0 + jnp.exp(-g)) * both[:, unit : 2 * unit]).astype(BF16)
            for i in range(1, n_d):
                hid_copy(b, i, True).start()

        @pl.when(t > 1)
        def _():
            b = t - 2
            for i in range(1, n_d):
                hid_copy(b, i, False).wait_recv()
            hidden = jnp.concatenate([hid[b, p] for p in range(n_d)], axis=1)
            result = dot(hidden, wd[...]).reshape(N_X, cap, width)

            @pl.when(b == 0)
            def _():
                own[...] = result

            @pl.when(b > 0)
            def _():
                for h in range(N_X):

                    @pl.when(b == 1)
                    def _():
                        rs_out[b, h] = result[h].astype(BF16)

                    @pl.when(b > 1)
                    def _():
                        rs_wait(b, h)
                        rs_out[b, h] = (result[h] + rs_in[b, h].astype(F32)).astype(BF16)

                    rs_copy(b, h).start()

        return carry

    lax.fori_loop(0, n_y + 2, tick, 0)

    other = 1 - xh
    rs_wait(n_y, other)
    xr_out[...] = (own[other] + rs_in[n_y, other].astype(F32)).astype(BF16)
    xr_copy = remote(xr_out, xr_in, xr_s, xr_r, section=across)
    xr_copy.start()
    rs_wait(n_y, xh)
    answer = own[xh] + rs_in[n_y, xh].astype(F32)
    xr_copy.wait_recv()
    answer = answer + xr_in[...].astype(F32)
    for e in range(n_e):
        top, below = pack(answer[:, e * n_feat : (e + 1) * n_feat])
        bk_out[e, 0:cap, :] = top.astype(BF16)
        bk_out[e, cap : cap + low, :] = below.astype(BF16)
    for i in order:
        z_copy(bk_out, bk_in, bk_s, bk_r, i, True).start()
    bk_in[z] = bk_out[z]
    for i in order[::-1]:
        z_copy(bk_out, bk_in, bk_s, bk_r, i, False).wait_recv()
    back_top = bk_in[:, 0:cap, :].reshape(n_e * cap, LANES)
    back_low = bk_in[:, cap : cap + low, :].reshape(n_e * low, LANES)
    edge = n_feat - LANES
    out_ref[0:LANES, :] = (
        tok_ref[0:LANES, :].astype(F32) + dot_first(back_top, mix_top[0]) + dot_first(back_top, mix_top[1])
    ).astype(BF16)
    low_a = dot_first(back_low, mix_low[0]) + dot_first(back_low, mix_low[1])
    low_b = dot_first(back_low, mix_low[2]) + dot_first(back_low, mix_low[3])
    out_ref[LANES:n_feat, :] = (
        tok_ref[LANES:n_feat, :].astype(F32) + low_a[0:edge] + low_b[edge : 2 * edge]
    ).astype(BF16)

    for i in order:
        z_copy(go, got, go_s, go_r, i, True).wait_send()
        z_copy(bk_out, bk_in, bk_s, bk_r, i, True).wait_send()
    for i in range(1, n_d):
        d_copy(ss_out, ss_in, ss_s, ss_r, i, True).wait_send()
    x_copy.wait_send()
    xr_copy.wait_send()

    def finish(b, carry):
        for i in range(1, n_d):
            part_copy(b, i, True).wait_send()
            hid_copy(b, i, True).wait_send()
        for h in range(N_X):

            @pl.when(b < n_y - 1)
            def _():
                ag_copy(b, h).wait_send()

            @pl.when(b > 0)
            def _():
                rs_copy(b, h).wait_send()

        return carry

    lax.fori_loop(0, n_y, finish, 0)


def local(tokens, norm_gain, routes, gates, w_gate, w_up, w_down):
    n_tok, n_feat = tokens.shape
    n_e = lax.axis_size("expert")
    n_d = lax.axis_size("dp")
    n_y = lax.axis_size("section") // N_X
    cap = min(n_tok, max(2, 3 * n_tok // n_e))
    half = cap // 2
    low = half + (-half % 16)
    width = n_feat * n_e
    units = w_gate.shape[2]
    unit = units // n_d
    rows = N_X * cap
    dma = pltpu.SemaphoreType.DMA
    vmem = pl.BlockSpec(memory_space=pltpu.VMEM)
    far = pl.BlockSpec(memory_space=pl.ANY)
    scratch = [
        pltpu.VMEM((width, units), BF16),
        pltpu.VMEM((width, units), BF16),
        pltpu.VMEM((units, width), BF16),
        dma((3,)),
        pltpu.VMEM((2, n_e * cap, n_tok), BF16),
        pltpu.VMEM((4, n_e * low, n_tok), BF16),
        pltpu.VMEM((n_e, cap + low, LANES), BF16),
        pltpu.VMEM((n_e, cap + low, LANES), BF16),
        pltpu.VMEM((8, LANES), F32),
        pltpu.VMEM((n_d, 8, LANES), F32),
        pltpu.VMEM((n_y, N_X, cap, width), BF16),
        pltpu.VMEM((n_y, n_d, rows, 2 * unit), BF16),
        pltpu.VMEM((n_y, n_d, rows, 2 * unit), BF16),
        pltpu.VMEM((n_y, n_d, rows, unit), BF16),
        pltpu.VMEM((n_y, N_X, cap, width), BF16),
        pltpu.VMEM((n_y + 1, N_X, cap, width), BF16),
        pltpu.VMEM((N_X, cap, width), F32),
        pltpu.VMEM((cap, width), BF16),
        pltpu.VMEM((cap, width), BF16),
        pltpu.VMEM((n_e, cap + low, LANES), BF16),
        pltpu.VMEM((n_e, cap + low, LANES), BF16),
        dma((n_e,)),
        dma((n_e,)),
        dma((n_d,)),
        dma((n_d,)),
        dma,
        dma,
        dma((n_y, N_X)),
        dma((n_y, N_X)),
        dma((n_y, n_d)),
        dma((n_y, n_d)),
        dma((n_y, n_d)),
        dma((n_y, n_d)),
        dma((n_y, N_X)),
        dma((n_y + 1, N_X)),
        dma,
        dma,
        dma((n_e,)),
        dma((n_e,)),
    ]
    mixed = pl.pallas_call(
        functools.partial(kernel, (n_y, n_e, n_d, cap)),
        out_shape=jax.ShapeDtypeStruct((n_feat, n_tok), BF16),
        in_specs=[vmem] * 4 + [far] * 3,
        out_specs=vmem,
        scratch_shapes=scratch,
        compiler_params=pltpu.CompilerParams(
            collective_id=0, has_side_effects=True, vmem_limit_bytes=48 * 1024 * 1024
        ),
        name="moe_layer",
    )(tokens.T, norm_gain.reshape(1, n_feat), routes.T, gates.T, w_gate, w_up, w_down)
    return mixed.T


def solution(mesh):
    in_specs = (
        P("section", ("dp", "expert")),
        P(("dp", "expert")),
        P("section", None),
        P("section", None),
        P("expert", "dp", "section"),
        P("expert", "dp", "section"),
        P("expert", "section", "dp"),
    )
    out_specs = P("section", ("dp", "expert"))
    return jax.shard_map(local, mesh=mesh, in_specs=in_specs, out_specs=out_specs, check_vma=False)
```

```python
import functools

import jax
import jax.numpy as jnp
from jax import lax
from jax.experimental import pallas as pl
from jax.experimental.pallas import tpu as pltpu
from jax.sharding import PartitionSpec as P

D = 6144
EPS = 1e-05
N_X = 2
F32 = jnp.float32
BF16 = jnp.bfloat16
LANES = 128
CHUNKS = 4


def dot(a, b):
    return jnp.dot(a, b, preferred_element_type=F32)


def dot_last(a, b):
    return lax.dot_general(a, b, (((1,), (1,)), ((), ())), preferred_element_type=F32)


def dot_first(a, b):
    return lax.dot_general(a, b, (((0,), (0,)), ((), ())), preferred_element_type=F32)


def split3(v):
    high = v.astype(BF16).astype(F32)
    rest = v - high
    mid = rest.astype(BF16).astype(F32)
    return high, mid, rest - mid


def pack(rows):
    half = rows.shape[0] // 2
    tail = rows[:, LANES:]
    return rows[:, :LANES], jnp.concatenate([tail[:half], tail[half:]], axis=1)


def kernel(
    sizes,
    tok_hbm,
    gain_hbm,
    routes_hbm,
    gates_hbm,
    wg_hbm,
    wu_hbm,
    wd_hbm,
    out_ref,
    tok_ref,
    gain_ref,
    routes_ref,
    gates_ref,
    wg,
    wu,
    wd,
    w_sem,
    mix_top,
    mix_low,
    go,
    got,
    ss_out,
    ss_in,
    sc,
    ag,
    part_out,
    part_in,
    hid,
    rs_out,
    rs_in,
    own,
    res,
    xr_out,
    xr_in,
    bk_out,
    bk_in,
    go_s,
    go_r,
    ss_s,
    ss_r,
    sx_s,
    sx_r,
    sc_s,
    sc_r,
    x_s,
    x_r,
    ag_s,
    ag_r,
    part_s,
    part_r,
    hid_s,
    hid_r,
    rs_s,
    rs_r,
    xr_s,
    xr_r,
    bk_s,
    bk_r,
):
    n_y, n_e, n_d, cap, n_c = sizes
    half = cap // 2
    low = half + 8
    n_feat, n_tok = tok_ref.shape
    edge = n_feat - LANES
    width = n_feat * n_e
    wide = width // n_c
    per = n_e // n_c
    rows = N_X * cap
    sec = lax.axis_index("section")
    z = lax.axis_index("expert")
    d = lax.axis_index("dp")
    xh = lax.div(sec, n_y)
    y = lax.rem(sec, n_y)
    up = xh * n_y + lax.rem(y + 1, n_y)
    down = xh * n_y + lax.rem(y + n_y - 1, n_y)
    across = (1 - xh) * n_y + y
    mine = lax.div(z, per)
    spread = sorted(range(n_c), key=lambda i: min(i, n_c - i))
    near_first = [lax.rem(mine + i, n_c) for i in spread]
    far_first = near_first[::-1]

    def ring(h):
        return xh * n_y + lax.rem(y + 1 + h * (n_y - 2), n_y)

    def remote(src, dst, send, recv, **where):
        return pltpu.make_async_remote_copy(
            src_ref=src,
            dst_ref=dst,
            send_sem=send,
            recv_sem=recv,
            device_id=where,
            device_id_type=pl.DeviceIdType.MESH,
        )

    barrier = pltpu.get_barrier_semaphore()

    def greet(**where):
        pl.semaphore_signal(barrier, inc=1, device_id=where, device_id_type=pl.DeviceIdType.MESH)

    order = sorted(range(1, n_e), key=lambda i: -min(i, n_e - i))
    for i in order:
        greet(expert=lax.rem(z + i, n_e))
    for to in (across, up, down):
        greet(section=to)
    for i in range(1, n_d):
        greet(dp=lax.rem(d + i, n_d))

    small = [
        pltpu.make_async_copy(src, dst, w_sem.at[i])
        for i, (src, dst) in enumerate(
            ((routes_hbm, routes_ref), (gates_hbm, gates_ref), (tok_hbm, tok_ref), (gain_hbm, gain_ref))
        )
    ]
    loads = [
        pltpu.make_async_copy(src.at[0], dst, w_sem.at[4 + i])
        for i, (src, dst) in enumerate(((wg_hbm, wg), (wu_hbm, wu), (wd_hbm, wd)))
    ]
    for load in small + loads:
        load.start()
    for load in small:
        load.wait()

    first = routes_ref[0:1, :]
    second = routes_ref[1:2, :]
    expert_ids = lax.broadcasted_iota(jnp.int32, (n_e, n_tok), 0)
    named = (first == expert_ids) | (second == expert_ids)
    earlier = (
        lax.broadcasted_iota(jnp.int32, (n_tok, n_tok), 0) < lax.broadcasted_iota(jnp.int32, (n_tok, n_tok), 1)
    )
    count = dot(jnp.where(named, 1.0, 0.0).astype(BF16), jnp.where(earlier, 1.0, 0.0).astype(BF16))
    slot = jnp.where(named, count, -1.0)
    weight = jnp.where(first == expert_ids, gates_ref[0:1, :], gates_ref[1:2, :])
    number = lax.broadcasted_iota(jnp.int32, (LANES, n_tok), 0).astype(F32)
    low_row = lax.broadcasted_iota(jnp.int32, (low, n_tok), 0)
    low_number = jnp.where(low_row < half, low_row, 4 * cap).astype(F32)
    picks = [jnp.where(slot[e : e + 1, :] == number, 1.0, 0.0) for e in range(n_e)]
    lows_a = [jnp.where(slot[e : e + 1, :] == low_number, 1.0, 0.0) for e in range(n_e)]
    lows_b = [jnp.where(slot[e : e + 1, :] == low_number + half, 1.0, 0.0) for e in range(n_e)]

    def stacked(parts):
        return jnp.concatenate([part.astype(BF16) for part in parts], axis=0)

    tok = tok_ref[...]
    tail = tok[LANES:]
    blank = jnp.zeros_like(tail)
    gain = gain_ref[...]
    gain_tail = gain[:, LANES:]
    sent_top = dot_last(stacked([p[:cap] for p in picks]), tok[:LANES]) * gain[:, :LANES]
    sent_low = (
        dot_last(stacked(lows_a), jnp.concatenate([tail, blank], axis=0))
        + dot_last(stacked(lows_b), jnp.concatenate([blank, tail], axis=0))
    ) * jnp.concatenate([gain_tail, gain_tail], axis=1)
    tok32 = tok.astype(F32)
    squares = split3(jnp.sum(tok32 * tok32, axis=0, keepdims=True))
    squares = jnp.concatenate(list(squares) + [jnp.zeros((5, n_tok), F32)], axis=0).astype(BF16)
    sent_squares = dot_last(squares, stacked(picks))
    go[:, 0:cap, :] = sent_top.astype(BF16).reshape(n_e, cap, LANES)
    for e in range(n_e):
        go[e, cap : cap + low, :] = jnp.concatenate(
            [sent_low[e * low : e * low + half], sent_squares[:, e * LANES : (e + 1) * LANES]], axis=0
        ).astype(BF16)

    pl.semaphore_wait(barrier, n_e - 1 + n_d - 1 + 3)

    def z_copy(src, dst, send, recv, i, outgoing):
        to = lax.rem(z + i, n_e)
        at = z if outgoing else to
        return remote(src.at[to], dst.at[at], send.at[to], recv.at[at], expert=to)

    for i in order:
        z_copy(go, got, go_s, go_r, i, True).start()
    got[z] = go[z]

    def x_copy(c, outgoing):
        h = xh if outgoing else 1 - xh
        return remote(ag.at[0, h, c], ag.at[0, h, c], x_s.at[c], x_r.at[c], section=across)

    def ag_copy(b, h, c):
        return remote(ag.at[b, h, c], ag.at[b + 1, h, c], ag_s.at[b, h, c], ag_r.at[b + 1, h, c], section=ring(h))

    def ag_wait(b, h, c):
        remote(ag.at[b, h, c], ag.at[b, h, c], ag_s.at[b, h, c], ag_r.at[b, h, c], section=ring(h)).wait_recv()

    for e in range(n_e):
        w = weight[e : e + 1, :]
        for part, store, lead, size in (
            (picks[e][:cap], mix_top, 0, cap),
            (lows_a[e], mix_low, 0, low),
            (lows_b[e], mix_low, 2, low),
        ):
            value = part * w
            high = value.astype(BF16)
            store[lead, e * size : (e + 1) * size, :] = high
            store[lead + 1, e * size : (e + 1) * size, :] = (value - high.astype(F32)).astype(BF16)

    row_squares = jnp.zeros((1, LANES), F32)
    for c in near_first:
        pieces = []
        for k in range(per):
            zp = c * per + k

            @pl.when(zp != z)
            def _():
                remote(go.at[zp], got.at[zp], go_s.at[zp], go_r.at[zp], expert=zp).wait_recv()

            block = got[zp].astype(F32)
            below = block[cap : cap + half]
            pieces.append(
                jnp.concatenate(
                    [block[:cap], jnp.concatenate([below[:, :edge], below[:, edge : 2 * edge]], axis=0)], axis=1
                )
            )
            terms = block[cap + half : cap + half + 8]
            row_squares = row_squares + (terms[0:1] + terms[1:2] + terms[2:3])
        ag[0, xh, c] = jnp.concatenate(pieces, axis=1).astype(BF16)
        x_copy(c, True).start()
        ag_copy(0, xh, c).start()

    def d_copy(src, dst, send, recv, i, outgoing):
        to = lax.rem(d + i, n_d)
        at = d if outgoing else to
        return remote(src, dst.at[at], send.at[to], recv.at[at], dp=to)

    ss_out[...] = jnp.broadcast_to(row_squares, ss_out.shape)
    for i in range(1, n_d):
        d_copy(ss_out, ss_in, ss_s, ss_r, i, True).start()
    for c in near_first:
        x_copy(c, False).wait_recv()
        ag_copy(0, 1 - xh, c).start()
    total = row_squares
    for i in range(1, n_d):
        d_copy(ss_out, ss_in, ss_s, ss_r, i, False).wait_recv()
        total = total + ss_in[lax.rem(d + i, n_d)][0:1, :]
    sc[0, xh] = jnp.broadcast_to(lax.rsqrt(total / (n_d * width) + EPS), ss_out.shape)
    sx_copy = remote(sc.at[0, xh], sc.at[0, xh], sx_s, sx_r, section=across)
    sx_copy.start()
    for load in loads:
        load.wait()

    def sc_copy(b, h):
        return remote(sc.at[b, h], sc.at[b + 1, h], sc_s.at[b, h], sc_r.at[b + 1, h], section=ring(h))

    def part_copy(b, i, outgoing):
        to = lax.rem(d + i, n_d)
        at = d if outgoing else to
        return remote(part_out.at[b, to], part_in.at[b, at], part_s.at[b, to], part_r.at[b, at], dp=to)

    def hid_copy(b, i, outgoing):
        to = lax.rem(d + i, n_d)
        at = d if outgoing else to
        return remote(hid.at[b, d], hid.at[b, at], hid_s.at[b, to], hid_r.at[b, at], dp=to)

    def rs_copy(b, h, c):
        return remote(
            rs_out.at[b, h, c], rs_in.at[b + 1, h, c], rs_s.at[b, h, c], rs_r.at[b + 1, h, c], section=ring(h)
        )

    def rs_wait(b, h, c):
        remote(rs_in.at[b, h, c], rs_in.at[b, h, c], rs_s.at[0, h, c], rs_r.at[b, h, c], section=ring(h)).wait_recv()

    unit = wg.shape[1] // n_d
    eye = lax.broadcasted_iota(jnp.int32, (cap, LANES), 0) == lax.broadcasted_iota(jnp.int32, (cap, LANES), 1)

    def tick(t, carry):
        @pl.when(t < n_y)
        def _():
            @pl.when(t > 0)
            def _():
                for c in near_first:
                    for h in range(N_X):
                        ag_wait(t, h, c)

                        @pl.when(t < n_y - 1)
                        def _():
                            ag_copy(t, h, c).start()

            block = jnp.concatenate([ag[t, :, c].reshape(rows, wide) for c in range(n_c)], axis=1)
            gate = dot(block, wg[...]).astype(BF16)
            upper = dot(block, wu[...]).astype(BF16)
            for p in range(n_d):
                part_out[t, p, :, 0:unit] = gate[:, p * unit : (p + 1) * unit]
                part_out[t, p, :, unit : 2 * unit] = upper[:, p * unit : (p + 1) * unit]
            for i in range(1, n_d):
                part_copy(t, i, True).start()

        @pl.when((t > 0) & (t < n_y + 1))
        def _():
            b = t - 1

            @pl.when(b == 0)
            def _():
                remote(sc.at[0, 1 - xh], sc.at[0, 1 - xh], sx_s, sx_r, section=across).wait_recv()

            scales = []
            for h in range(N_X):

                @pl.when(b > 0)
                def _():
                    remote(sc.at[b, h], sc.at[b, h], sc_s.at[0, h], sc_r.at[b, h], section=ring(h)).wait_recv()

                @pl.when(b < n_y - 1)
                def _():
                    sc_copy(b, h).start()

                scales.append(jnp.sum(jnp.where(eye, sc[b, h][0:1, :], 0.0), axis=1, keepdims=True))
            both = part_out[b, d].astype(F32)
            for i in range(1, n_d):
                part_copy(b, i, False).wait_recv()
                both = both + part_in[b, lax.rem(d + i, n_d)].astype(F32)
            both = both * jnp.concatenate(scales, axis=0)
            g = both[:, 0:unit]
            hid[b, d] = (g / (1.0 + jnp.exp(-g)) * both[:, unit : 2 * unit]).astype(BF16)
            for i in range(1, n_d):
                hid_copy(b, i, True).start()

        @pl.when(t > 1)
        def _():
            b = t - 2
            for i in range(1, n_d):
                hid_copy(b, i, False).wait_recv()
            hidden = jnp.concatenate([hid[b, p] for p in range(n_d)], axis=1)
            result = dot(hidden, wd[...])

            def keep(ref):
                for h in range(N_X):
                    for c in range(n_c):
                        ref[h, c] = result[h * cap : (h + 1) * cap, c * wide : (c + 1) * wide]

            @pl.when(b == 0)
            def _():
                keep(own)

            @pl.when(b > 0)
            def _():
                keep(res)
                for c in far_first:
                    for h in range(N_X):

                        @pl.when(b == 1)
                        def _():
                            rs_out[b, h, c] = res[h, c].astype(BF16)

                        @pl.when(b > 1)
                        def _():
                            rs_wait(b, h, c)
                            rs_out[b, h, c] = (res[h, c] + rs_in[b, h, c].astype(F32)).astype(BF16)

                        rs_copy(b, h, c).start()

        return carry

    lax.fori_loop(0, n_y + 2, tick, 0)

    other = 1 - xh

    def xr_copy(c):
        return remote(xr_out.at[c], xr_in.at[c], xr_s.at[c], xr_r.at[c], section=across)

    for c in far_first:
        rs_wait(n_y, other, c)
        xr_out[c] = (own[other, c] + rs_in[n_y, other, c].astype(F32)).astype(BF16)
        xr_copy(c).start()
    for c in far_first:
        rs_wait(n_y, xh, c)
        answer = own[xh, c] + rs_in[n_y, xh, c].astype(F32)
        xr_copy(c).wait_recv()
        answer = answer + xr_in[c].astype(F32)
        for k in range(per):
            zp = c * per + k
            top, below = pack(answer[:, k * n_feat : (k + 1) * n_feat])
            bk_out[zp, 0:cap, :] = top.astype(BF16)
            bk_out[zp, cap : cap + low, :] = jnp.concatenate([below, jnp.zeros((8, LANES), F32)], axis=0).astype(BF16)

            @pl.when(zp != z)
            def _():
                remote(bk_out.at[zp], bk_in.at[z], bk_s.at[zp], bk_r.at[z], expert=zp).start()

    bk_in[z] = bk_out[z]
    for i in order[::-1]:
        z_copy(bk_out, bk_in, bk_s, bk_r, i, False).wait_recv()
    back_top = bk_in[:, 0:cap, :].reshape(n_e * cap, LANES)
    back_low = bk_in[:, cap : cap + low, :].reshape(n_e * low, LANES)
    out_ref[0:LANES, :] = (
        tok_ref[0:LANES, :].astype(F32) + dot_first(back_top, mix_top[0]) + dot_first(back_top, mix_top[1])
    ).astype(BF16)
    low_a = dot_first(back_low, mix_low[0]) + dot_first(back_low, mix_low[1])
    low_b = dot_first(back_low, mix_low[2]) + dot_first(back_low, mix_low[3])
    out_ref[LANES:n_feat, :] = (
        tok_ref[LANES:n_feat, :].astype(F32) + low_a[0:edge] + low_b[edge : 2 * edge]
    ).astype(BF16)

    for i in order:
        z_copy(go, got, go_s, go_r, i, True).wait_send()
        z_copy(bk_out, bk_in, bk_s, bk_r, i, True).wait_send()
    for i in range(1, n_d):
        d_copy(ss_out, ss_in, ss_s, ss_r, i, True).wait_send()
    sx_copy.wait_send()
    for c in range(n_c):
        x_copy(c, True).wait_send()
        xr_copy(c).wait_send()

    def finish(b, carry):
        for i in range(1, n_d):
            part_copy(b, i, True).wait_send()
            hid_copy(b, i, True).wait_send()
        for h in range(N_X):

            @pl.when(b < n_y - 1)
            def _():
                sc_copy(b, h).wait_send()
                for c in range(n_c):
                    ag_copy(b, h, c).wait_send()

            @pl.when(b > 0)
            def _():
                for c in range(n_c):
                    rs_copy(b, h, c).wait_send()

        return carry

    lax.fori_loop(0, n_y, finish, 0)


def local(tokens, norm_gain, routes, gates, w_gate, w_up, w_down):
    n_tok, n_feat = tokens.shape
    n_e = lax.axis_size("expert")
    n_d = lax.axis_size("dp")
    n_y = lax.axis_size("section") // N_X
    n_c = min(CHUNKS, n_e)
    cap = min(n_tok, max(2, 3 * n_tok // n_e))
    low = cap // 2 + 8
    width = n_feat * n_e
    wide = width // n_c
    units = w_gate.shape[2]
    unit = units // n_d
    rows = N_X * cap
    dma = pltpu.SemaphoreType.DMA
    far = pl.BlockSpec(memory_space=pl.ANY)
    scratch = [
        pltpu.VMEM((n_feat, n_tok), BF16),
        pltpu.VMEM((1, n_feat), F32),
        pltpu.VMEM((2, n_tok), jnp.int32),
        pltpu.VMEM((2, n_tok), F32),
        pltpu.VMEM((width, units), BF16),
        pltpu.VMEM((width, units), BF16),
        pltpu.VMEM((units, width), BF16),
        dma((7,)),
        pltpu.VMEM((2, n_e * cap, n_tok), BF16),
        pltpu.VMEM((4, n_e * low, n_tok), BF16),
        pltpu.VMEM((n_e, cap + low, LANES), BF16),
        pltpu.VMEM((n_e, cap + low, LANES), BF16),
        pltpu.VMEM((8, LANES), F32),
        pltpu.VMEM((n_d, 8, LANES), F32),
        pltpu.VMEM((n_y, N_X, 8, LANES), F32),
        pltpu.VMEM((n_y, N_X, n_c, cap, wide), BF16),
        pltpu.VMEM((n_y, n_d, rows, 2 * unit), BF16),
        pltpu.VMEM((n_y, n_d, rows, 2 * unit), BF16),
        pltpu.VMEM((n_y, n_d, rows, unit), BF16),
        pltpu.VMEM((n_y, N_X, n_c, cap, wide), BF16),
        pltpu.VMEM((n_y + 1, N_X, n_c, cap, wide), BF16),
        pltpu.VMEM((N_X, n_c, cap, wide), F32),
        pltpu.VMEM((N_X, n_c, cap, wide), F32),
        pltpu.VMEM((n_c, cap, wide), BF16),
        pltpu.VMEM((n_c, cap, wide), BF16),
        pltpu.VMEM((n_e, cap + low, LANES), BF16),
        pltpu.VMEM((n_e, cap + low, LANES), BF16),
        dma((n_e,)),
        dma((n_e,)),
        dma((n_d,)),
        dma((n_d,)),
        dma,
        dma,
        dma((n_y, N_X)),
        dma((n_y, N_X)),
        dma((n_c,)),
        dma((n_c,)),
        dma((n_y, N_X, n_c)),
        dma((n_y, N_X, n_c)),
        dma((n_y, n_d)),
        dma((n_y, n_d)),
        dma((n_y, n_d)),
        dma((n_y, n_d)),
        dma((n_y, N_X, n_c)),
        dma((n_y + 1, N_X, n_c)),
        dma((n_c,)),
        dma((n_c,)),
        dma((n_e,)),
        dma((n_e,)),
    ]
    mixed = pl.pallas_call(
        functools.partial(kernel, (n_y, n_e, n_d, cap, n_c)),
        out_shape=jax.ShapeDtypeStruct((n_feat, n_tok), BF16),
        in_specs=[far] * 7,
        out_specs=pl.BlockSpec(memory_space=pltpu.VMEM),
        scratch_shapes=scratch,
        compiler_params=pltpu.CompilerParams(
            collective_id=0, has_side_effects=True, vmem_limit_bytes=64 * 1024 * 1024
        ),
        name="moe_layer",
    )(tokens.T, norm_gain.reshape(1, n_feat), routes.T, gates.T, w_gate, w_up, w_down)
    return mixed.T


def solution(mesh):
    in_specs = (
        P("section", ("dp", "expert")),
        P(("dp", "expert")),
        P("section", None),
        P("section", None),
        P("expert", "dp", "section"),
        P("expert", "dp", "section"),
        P("expert", "section", "dp"),
    )
    out_specs = P("section", ("dp", "expert"))
    return jax.shard_map(local, mesh=mesh, in_specs=in_specs, out_specs=out_specs, check_vma=False)
```

```python
import functools

import jax
import jax.numpy as jnp
from jax import lax
from jax.experimental import pallas as pl
from jax.experimental.pallas import tpu as pltpu
from jax.sharding import PartitionSpec as P

D = 6144
EPS = 1e-05
N_X = 2
F32 = jnp.float32
BF16 = jnp.bfloat16
LANES = 128
CHUNKS = 4
RING = 3
TURN = 4


def dot(a, b):
    return jnp.dot(a, b, preferred_element_type=F32)


def dot_last(a, b):
    return lax.dot_general(a, b, (((1,), (1,)), ((), ())), preferred_element_type=F32)


def dot_first(a, b):
    return lax.dot_general(a, b, (((0,), (0,)), ((), ())), preferred_element_type=F32)


def split3(v):
    high = v.astype(BF16).astype(F32)
    rest = v - high
    mid = rest.astype(BF16).astype(F32)
    return high, mid, rest - mid


def pack(rows):
    half = rows.shape[0] // 2
    tail = rows[:, LANES:]
    return rows[:, :LANES], jnp.concatenate([tail[:half], tail[half:]], axis=1)


def kernel(
    sizes,
    tok_hbm,
    gain_hbm,
    routes_hbm,
    gates_hbm,
    wg_hbm,
    wu_hbm,
    wd_hbm,
    out_ref,
    tok_ref,
    gain_ref,
    routes_ref,
    gates_ref,
    wg,
    wu,
    wd,
    w_sem,
    mix_top,
    mix_low,
    go,
    got,
    ss_out,
    ss_in,
    sc,
    ag,
    part_out,
    part_in,
    hid,
    hid_in,
    own,
    res,
    rs_out,
    rs_in,
    xr_out,
    xr_in,
    bk_out,
    bk_in,
    go_s,
    go_r,
    ss_s,
    ss_r,
    sx_s,
    sx_r,
    sc_s,
    sc_r,
    x_s,
    x_r,
    ag_s,
    ag_r,
    part_s,
    part_r,
    hid_s,
    hid_r,
    rs_s,
    rs_r,
    xr_s,
    xr_r,
    bk_s,
    bk_r,
):
    n_y, n_e, n_d, cap, n_c = sizes
    half = cap // 2
    low = half + 8
    n_feat, n_tok = tok_ref.shape
    edge = n_feat - LANES
    width = n_feat * n_e
    wide = width // n_c
    per = n_e // n_c
    rows = N_X * cap
    sec = lax.axis_index("section")
    z = lax.axis_index("expert")
    d = lax.axis_index("dp")
    xh = lax.div(sec, n_y)
    y = lax.rem(sec, n_y)
    up = xh * n_y + lax.rem(y + 1, n_y)
    down = xh * n_y + lax.rem(y + n_y - 1, n_y)
    across = (1 - xh) * n_y + y
    mine = lax.div(z, per)
    spread = sorted(range(n_c), key=lambda i: min(i, n_c - i))
    near_first = [lax.rem(mine + i, n_c) for i in spread]
    far_first = near_first[::-1]

    def ring(h):
        return xh * n_y + lax.rem(y + 1 + h * (n_y - 2), n_y)

    def remote(src, dst, send, recv, **where):
        return pltpu.make_async_remote_copy(
            src_ref=src,
            dst_ref=dst,
            send_sem=send,
            recv_sem=recv,
            device_id=where,
            device_id_type=pl.DeviceIdType.MESH,
        )

    barrier = pltpu.get_barrier_semaphore()

    def greet(**where):
        pl.semaphore_signal(barrier, inc=1, device_id=where, device_id_type=pl.DeviceIdType.MESH)

    order = sorted(range(1, n_e), key=lambda i: -min(i, n_e - i))
    for i in order:
        greet(expert=lax.rem(z + i, n_e))
    for to in (across, up, down):
        greet(section=to)
    for i in range(1, n_d):
        greet(dp=lax.rem(d + i, n_d))

    small = [
        pltpu.make_async_copy(src, dst, w_sem.at[i])
        for i, (src, dst) in enumerate(
            ((routes_hbm, routes_ref), (gates_hbm, gates_ref), (tok_hbm, tok_ref), (gain_hbm, gain_ref))
        )
    ]
    loads = [
        pltpu.make_async_copy(src.at[0], dst, w_sem.at[4 + i])
        for i, (src, dst) in enumerate(((wg_hbm, wg), (wu_hbm, wu), (wd_hbm, wd)))
    ]
    for load in small + loads:
        load.start()
    for load in small:
        load.wait()

    first = routes_ref[0:1, :]
    second = routes_ref[1:2, :]
    expert_ids = lax.broadcasted_iota(jnp.int32, (n_e, n_tok), 0)
    named = (first == expert_ids) | (second == expert_ids)
    earlier = (
        lax.broadcasted_iota(jnp.int32, (n_tok, n_tok), 0) < lax.broadcasted_iota(jnp.int32, (n_tok, n_tok), 1)
    )
    count = dot(jnp.where(named, 1.0, 0.0).astype(BF16), jnp.where(earlier, 1.0, 0.0).astype(BF16))
    slot = jnp.where(named, count, -1.0)
    weight = jnp.where(first == expert_ids, gates_ref[0:1, :], gates_ref[1:2, :])
    number = lax.broadcasted_iota(jnp.int32, (cap, n_tok), 0).astype(F32)
    picks = [jnp.where(slot[e : e + 1, :] == number, 1.0, 0.0) for e in range(n_e)]
    eye = lax.broadcasted_iota(jnp.int32, (cap, LANES), 0) == lax.broadcasted_iota(jnp.int32, (cap, LANES), 1)
    picked = dot_last(jnp.concatenate([p.astype(BF16) for p in picks], axis=0), tok_ref[...])
    squares = jnp.sum(picked * picked, axis=1, keepdims=True)
    picked = picked * gain_ref[...]
    for e in range(n_e):
        top, below = pack(picked[e * cap : (e + 1) * cap])
        go[e, 0:cap, :] = top.astype(BF16)
        terms = split3(jnp.sum(jnp.where(eye, squares[e * cap : (e + 1) * cap], 0.0), axis=0, keepdims=True))
        go[e, cap : cap + low, :] = jnp.concatenate(
            [below] + list(terms) + [jnp.zeros((5, LANES), F32)], axis=0
        ).astype(BF16)

    pl.semaphore_wait(barrier, n_e - 1 + n_d - 1 + 3)

    def z_copy(src, dst, send, recv, to):
        return remote(src.at[to], dst.at[z], send, recv, expert=to)

    for i in order:
        z_copy(go, got, go_s, go_r.at[z], lax.rem(z + i, n_e)).start()
    got[z] = go[z]

    def x_copy(c):
        return remote(ag.at[0, xh, c], ag.at[0, xh, c], x_s, x_r.at[c], section=across)

    def ag_copy(b, h, c):
        at = lax.rem(b, RING)
        return remote(
            ag.at[b, h, c], ag.at[b + 1, h, c], ag_s.at[at, h], ag_r.at[lax.rem(b + 1, RING), h, c], section=ring(h)
        )

    def ag_sent(b, h):
        remote(ag.at[b, h], ag.at[b, h], ag_s.at[lax.rem(b, RING), h], ag_r.at[0, h, 0], section=ring(h)).wait_send()

    def ag_wait(b, h, c):
        at = lax.rem(b, RING)
        remote(ag.at[b, h, c], ag.at[b, h, c], ag_s.at[at, h], ag_r.at[at, h, c], section=ring(h)).wait_recv()

    low_row = lax.broadcasted_iota(jnp.int32, (low, n_tok), 0)
    low_number = jnp.where(low_row < half, low_row, 4 * cap).astype(F32)
    for e in range(n_e):
        mark = slot[e : e + 1, :]
        w = weight[e : e + 1, :]
        for part, store, lead, size in (
            (picks[e], mix_top, 0, cap),
            (jnp.where(mark == low_number, 1.0, 0.0), mix_low, 0, low),
            (jnp.where(mark == low_number + half, 1.0, 0.0), mix_low, 2, low),
        ):
            value = part * w
            high = value.astype(BF16)
            store[lead, e * size : (e + 1) * size, :] = high
            store[lead + 1, e * size : (e + 1) * size, :] = (value - high.astype(F32)).astype(BF16)

    row_squares = jnp.zeros((1, LANES), F32)
    for c in near_first:
        pieces = []
        for k in range(per):
            zp = c * per + k

            @pl.when(zp != z)
            def _():
                remote(go.at[zp], got.at[zp], go_s, go_r.at[zp], expert=zp).wait_recv()

            block = got[zp].astype(F32)
            below = block[cap : cap + half]
            pieces.append(
                jnp.concatenate(
                    [block[:cap], jnp.concatenate([below[:, :edge], below[:, edge : 2 * edge]], axis=0)], axis=1
                )
            )
            terms = block[cap + half : cap + half + 8]
            row_squares = row_squares + (terms[0:1] + terms[1:2] + terms[2:3])
        ag[0, xh, c] = jnp.concatenate(pieces, axis=1).astype(BF16)
        x_copy(c).start()
        ag_copy(0, xh, c).start()

    def d_copy(src, dst, send, recv, i):
        return remote(src, dst.at[i - 1], send, recv, dp=lax.rem(d + i, n_d))

    def d_all(dst, send, recv):
        return remote(dst, dst, send, recv, dp=lax.rem(d + 1, n_d))

    ss_out[...] = jnp.broadcast_to(row_squares, ss_out.shape)
    for i in range(1, n_d):
        d_copy(ss_out, ss_in, ss_s, ss_r, i).start()
    for c in near_first:
        remote(ag.at[0, 1 - xh, c], ag.at[0, 1 - xh, c], x_s, x_r.at[c], section=across).wait_recv()
        ag_copy(0, 1 - xh, c).start()
    d_all(ss_in, ss_s, ss_r).wait_recv()
    total = row_squares
    for i in range(n_d - 1):
        total = total + ss_in[i][0:1, :]
    sc[0, xh] = jnp.broadcast_to(lax.rsqrt(total / (n_d * width) + EPS), ss_out.shape)
    sx_copy = remote(sc.at[0, xh], sc.at[0, xh], sx_s, sx_r, section=across)
    sx_copy.start()
    for load in loads:
        load.wait()

    def sc_copy(b, h):
        at = lax.rem(b, 2)
        return remote(sc.at[b, h], sc.at[b + 1, h], sc_s.at[at, h], sc_r.at[1 - at, h], section=ring(h))

    def part_copy(b, i):
        at = lax.rem(b, TURN)
        return d_copy(part_out.at[b, lax.rem(d + i, n_d)], part_in.at[b], part_s.at[at], part_r.at[at], i)

    def part_all(b):
        at = lax.rem(b, TURN)
        return d_all(part_in.at[b], part_s.at[at], part_r.at[at])

    def hid_copy(b, i):
        at = lax.rem(b, TURN)
        return d_copy(hid.at[b], hid_in.at[b], hid_s.at[at], hid_r.at[at], i)

    def hid_all(b):
        at = lax.rem(b, TURN)
        return d_all(hid_in.at[b], hid_s.at[at], hid_r.at[at])

    def rs_copy(b, h, c):
        return remote(
            rs_out.at[b, h, c],
            rs_in.at[b + 1, h, c],
            rs_s.at[lax.rem(b, RING), h],
            rs_r.at[lax.rem(b + 1, RING), h, c],
            section=ring(h),
        )

    def rs_wait(b, h, c):
        at = lax.rem(b, RING)
        remote(rs_in.at[b, h, c], rs_in.at[b, h, c], rs_s.at[at, h], rs_r.at[at, h, c], section=ring(h)).wait_recv()

    def rs_sent(b, h):
        some = rs_out.at[b, h]
        remote(some, some, rs_s.at[lax.rem(b, RING), h], rs_r.at[0, h, 0], section=ring(h)).wait_send()

    unit = wg.shape[1] // n_d

    def gate_up(b):
        @pl.when(b >= TURN)
        def _():
            part_all(b - TURN).wait_send()

        block = jnp.concatenate([ag[b, :, c].reshape(rows, wide) for c in range(n_c)], axis=1)
        gate = dot(block, wg[...]).astype(BF16)
        upper = dot(block, wu[...]).astype(BF16)
        for p in range(n_d):
            part_out[b, p, :, 0:unit] = gate[:, p * unit : (p + 1) * unit]
            part_out[b, p, :, unit : 2 * unit] = upper[:, p * unit : (p + 1) * unit]
        for i in range(1, n_d):
            part_copy(b, i).start()

    def hidden_units(b):
        @pl.when(b == 0)
        def _():
            remote(sc.at[0, 1 - xh], sc.at[0, 1 - xh], sx_s, sx_r, section=across).wait_recv()

        @pl.when(b > 0)
        def _():
            for h in range(N_X):
                remote(
                    sc.at[b, h], sc.at[b, h], sc_s.at[0, h], sc_r.at[lax.rem(b, 2), h], section=ring(h)
                ).wait_recv()

        @pl.when((b > 1) & (b < n_y - 1))
        def _():
            for h in range(N_X):
                sc_copy(b - 2, h).wait_send()

        @pl.when(b < n_y - 1)
        def _():
            for h in range(N_X):
                sc_copy(b, h).start()

        @pl.when(b >= TURN)
        def _():
            hid_all(b - TURN).wait_send()

        scales = [jnp.sum(jnp.where(eye, sc[b, h][0:1, :], 0.0), axis=1, keepdims=True) for h in range(N_X)]
        both = part_out[b, d].astype(F32)
        part_all(b).wait_recv()
        for i in range(n_d - 1):
            both = both + part_in[b, i].astype(F32)
        both = both * jnp.concatenate(scales, axis=0)
        g = both[:, 0:unit]
        hid[b] = (g / (1.0 + jnp.exp(-g)) * both[:, unit : 2 * unit]).astype(BF16)
        for i in range(1, n_d):
            hid_copy(b, i).start()

    def down_product(b):
        hid_all(b).wait_recv()
        parts = [hid[b]] + [hid_in[b, i] for i in range(n_d - 1)]
        columns = []
        for p in range(n_d):
            value = parts[0]
            for i in range(1, n_d):
                value = jnp.where(lax.rem(d + n_d - i, n_d) == p, parts[i], value)
            columns.append(value)
        result = dot(jnp.concatenate(columns, axis=1), wd[...])

        def keep(ref):
            for h in range(N_X):
                for c in range(n_c):
                    ref[h, c] = result[h * cap : (h + 1) * cap, c * wide : (c + 1) * wide]

        @pl.when(b == 0)
        def _():
            keep(own)

        @pl.when(b > 0)
        def _():
            keep(res)

    def add_on(b, c):
        for h in range(N_X):

            @pl.when(b == 1)
            def _():
                rs_out[b, h, c] = res[h, c].astype(BF16)

            @pl.when(b > 1)
            def _():
                rs_wait(b, h, c)
                rs_out[b, h, c] = (res[h, c] + rs_in[b, h, c].astype(F32)).astype(BF16)

            rs_copy(b, h, c).start()

    def step(t, carry):
        @pl.when(t <= n_y)
        def _():
            gate_up(t - 1)

        @pl.when((t < n_y - 1) & (t >= RING))
        def _():
            for h in range(N_X):
                ag_sent(t - RING, h)

        for j in range(n_c):
            c = near_first[j]

            @pl.when(t < n_y)
            def _():
                for h in range(N_X):
                    ag_wait(t, h, c)

                    @pl.when(t < n_y - 1)
                    def _():
                        ag_copy(t, h, c).start()

            if j == 0:

                @pl.when(t > 4)
                def _():
                    add_on(t - 4, far_first[n_c - 1])

            if j == 1:

                @pl.when((t > 2) & (t < n_y + 3))
                def _():
                    down_product(t - 3)

                @pl.when((t >= 4 + RING) & (t < n_y + 3))
                def _():
                    for h in range(N_X):
                        rs_sent(t - 3 - RING, h)

            if j >= 1:

                @pl.when((t > 3) & (t < n_y + 3))
                def _():
                    add_on(t - 3, far_first[j - 1])

            if j == 1:

                @pl.when((t > 1) & (t < n_y + 2))
                def _():
                    hidden_units(t - 2)

        return carry

    lax.fori_loop(1, n_y + 4, step, 0)

    other = 1 - xh

    def xr_copy(c):
        return remote(xr_out.at[c], xr_in.at[c], xr_s, xr_r.at[c], section=across)

    for c in far_first:
        rs_wait(n_y, other, c)
        xr_out[c] = (own[other, c] + rs_in[n_y, other, c].astype(F32)).astype(BF16)
        xr_copy(c).start()
    for c in far_first:
        rs_wait(n_y, xh, c)
        answer = own[xh, c] + rs_in[n_y, xh, c].astype(F32)
        xr_copy(c).wait_recv()
        answer = answer + xr_in[c].astype(F32)
        for k in range(per):
            zp = c * per + k
            top, below = pack(answer[:, k * n_feat : (k + 1) * n_feat])
            bk_out[zp, 0:cap, :] = top.astype(BF16)
            bk_out[zp, cap : cap + low, :] = jnp.concatenate([below, jnp.zeros((8, LANES), F32)], axis=0).astype(BF16)

            @pl.when(zp != z)
            def _():
                z_copy(bk_out, bk_in, bk_s, bk_r, zp).start()

    bk_in[z] = bk_out[z]

    def z_all(src, send, recv):
        some = src.at[pl.ds(0, n_e - 1)]
        return remote(some, some, send, recv, expert=lax.rem(z + 1, n_e))

    z_all(bk_in, bk_s, bk_r).wait_recv()
    back_top = bk_in[:, 0:cap, :].reshape(n_e * cap, LANES)
    back_low = bk_in[:, cap : cap + low, :].reshape(n_e * low, LANES)
    out_ref[0:LANES, :] = (
        tok_ref[0:LANES, :].astype(F32) + dot_first(back_top, mix_top[0]) + dot_first(back_top, mix_top[1])
    ).astype(BF16)
    low_a = dot_first(back_low, mix_low[0]) + dot_first(back_low, mix_low[1])
    low_b = dot_first(back_low, mix_low[2]) + dot_first(back_low, mix_low[3])
    out_ref[LANES:n_feat, :] = (
        tok_ref[LANES:n_feat, :].astype(F32) + low_a[0:edge] + low_b[edge : 2 * edge]
    ).astype(BF16)

    z_all(go, go_s, go_r.at[0]).wait_send()
    z_all(bk_out, bk_s, bk_r).wait_send()
    d_all(ss_in, ss_s, ss_r).wait_send()
    sx_copy.wait_send()
    remote(ag.at[0, xh], ag.at[0, xh], x_s, x_r.at[0], section=across).wait_send()
    remote(xr_out, xr_out, xr_s, xr_r.at[0], section=across).wait_send()
    for h in range(N_X):
        for b in range(max(0, n_y - 3), n_y - 1):
            sc_copy(b, h).wait_send()
        for b in range(max(0, n_y - 1 - RING), n_y - 1):
            ag_sent(b, h)
        for b in range(max(1, n_y - RING), n_y):
            rs_sent(b, h)
    for b in range(max(0, n_y - TURN), n_y):
        part_all(b).wait_send()
        hid_all(b).wait_send()


def local(tokens, norm_gain, routes, gates, w_gate, w_up, w_down):
    n_tok, n_feat = tokens.shape
    n_e = lax.axis_size("expert")
    n_d = lax.axis_size("dp")
    n_y = lax.axis_size("section") // N_X
    n_c = min(CHUNKS, n_e)
    cap = min(n_tok, max(2, 3 * n_tok // n_e))
    low = cap // 2 + 8
    width = n_feat * n_e
    wide = width // n_c
    units = w_gate.shape[2]
    unit = units // n_d
    rows = N_X * cap
    dma = pltpu.SemaphoreType.DMA
    far = pl.BlockSpec(memory_space=pl.ANY)
    scratch = [
        pltpu.VMEM((n_feat, n_tok), BF16),
        pltpu.VMEM((1, n_feat), F32),
        pltpu.VMEM((2, n_tok), jnp.int32),
        pltpu.VMEM((2, n_tok), F32),
        pltpu.VMEM((width, units), BF16),
        pltpu.VMEM((width, units), BF16),
        pltpu.VMEM((units, width), BF16),
        dma((7,)),
        pltpu.VMEM((2, n_e * cap, n_tok), BF16),
        pltpu.VMEM((4, n_e * low, n_tok), BF16),
        pltpu.VMEM((n_e, cap + low, LANES), BF16),
        pltpu.VMEM((n_e, cap + low, LANES), BF16),
        pltpu.VMEM((8, LANES), F32),
        pltpu.VMEM((n_d - 1, 8, LANES), F32),
        pltpu.VMEM((n_y, N_X, 8, LANES), F32),
        pltpu.VMEM((n_y, N_X, n_c, cap, wide), BF16),
        pltpu.VMEM((n_y, n_d, rows, 2 * unit), BF16),
        pltpu.VMEM((n_y, n_d - 1, rows, 2 * unit), BF16),
        pltpu.VMEM((n_y, rows, unit), BF16),
        pltpu.VMEM((n_y, n_d - 1, rows, unit), BF16),
        pltpu.VMEM((N_X, n_c, cap, wide), F32),
        pltpu.VMEM((N_X, n_c, cap, wide), F32),
        pltpu.VMEM((n_y, N_X, n_c, cap, wide), BF16),
        pltpu.VMEM((n_y + 1, N_X, n_c, cap, wide), BF16),
        pltpu.VMEM((n_c, cap, wide), BF16),
        pltpu.VMEM((n_c, cap, wide), BF16),
        pltpu.VMEM((n_e, cap + low, LANES), BF16),
        pltpu.VMEM((n_e, cap + low, LANES), BF16),
        dma,
        dma((n_e,)),
        dma,
        dma,
        dma,
        dma,
        dma((2, N_X)),
        dma((2, N_X)),
        dma,
        dma((n_c,)),
        dma((RING, N_X)),
        dma((RING, N_X, n_c)),
        dma((TURN,)),
        dma((TURN,)),
        dma((TURN,)),
        dma((TURN,)),
        dma((RING, N_X)),
        dma((RING, N_X, n_c)),
        dma,
        dma((n_c,)),
        dma,
        dma,
    ]
    mixed = pl.pallas_call(
        functools.partial(kernel, (n_y, n_e, n_d, cap, n_c)),
        out_shape=jax.ShapeDtypeStruct((n_feat, n_tok), BF16),
        in_specs=[far] * 7,
        out_specs=pl.BlockSpec(memory_space=pltpu.VMEM),
        scratch_shapes=scratch,
        compiler_params=pltpu.CompilerParams(
            collective_id=0, has_side_effects=True, vmem_limit_bytes=64 * 1024 * 1024
        ),
        name="moe_layer",
    )(tokens.T, norm_gain.reshape(1, n_feat), routes.T, gates.T, w_gate, w_up, w_down)
    return mixed.T


def solution(mesh):
    in_specs = (
        P("section", ("dp", "expert")),
        P(("dp", "expert")),
        P("section", None),
        P("section", None),
        P("expert", "dp", "section"),
        P("expert", "dp", "section"),
        P("expert", "section", "dp"),
    )
    out_specs = P("section", ("dp", "expert"))
    return jax.shard_map(local, mesh=mesh, in_specs=in_specs, out_specs=out_specs, check_vma=False)
```

```python
import functools

import jax
import jax.numpy as jnp
from jax import lax
from jax.experimental import pallas as pl
from jax.experimental.pallas import tpu as pltpu
from jax.sharding import PartitionSpec as P

D = 6144
EPS = 1e-05
N_X = 2
F32 = jnp.float32
BF16 = jnp.bfloat16
LANES = 128
CHUNKS = 4
RING = 3
TURN = 4
PAIR_AT, HIDDEN_AT, DOWN_AT = 1, 2, 3


def dot(a, b):
    return jnp.dot(a, b, preferred_element_type=F32)


def dot_last(a, b):
    return lax.dot_general(a, b, (((1,), (1,)), ((), ())), preferred_element_type=F32)


def dot_first(a, b):
    return lax.dot_general(a, b, (((0,), (0,)), ((), ())), preferred_element_type=F32)


def split3(v):
    high = v.astype(BF16).astype(F32)
    rest = v - high
    mid = rest.astype(BF16).astype(F32)
    return high, mid, rest - mid


def pack(rows):
    half = rows.shape[0] // 2
    tail = rows[:, LANES:]
    return rows[:, :LANES], jnp.concatenate([tail[:half], tail[half:]], axis=1)


def kernel(
    sizes,
    tok_hbm,
    gain_hbm,
    routes_hbm,
    gates_hbm,
    wg_hbm,
    wu_hbm,
    wd_hbm,
    out_ref,
    tok_ref,
    gain_ref,
    routes_ref,
    gates_ref,
    wg,
    wu,
    wd,
    w_sem,
    mix_top,
    mix_low,
    go,
    got,
    ss_out,
    ss_in,
    sc,
    ag,
    part_out,
    core_in,
    pair_out,
    pair_in,
    hid,
    own,
    res,
    cross_out,
    cross_in,
    rs_out,
    rs_in,
    xr_out,
    xr_in,
    bk_out,
    bk_in,
    go_s,
    go_r,
    ss_s,
    ss_r,
    sx_s,
    sx_r,
    sc_s,
    sc_r,
    x_s,
    x_r,
    ag_s,
    ag_r,
    ax_s,
    ax_r,
    core_s,
    core_r,
    pair_s,
    pair_r,
    hid_s,
    hid_r,
    rs_s,
    rs_r,
    rx_s,
    rx_r,
    xr_s,
    xr_r,
    bk_s,
    bk_r,
):
    n_y, n_e, n_d, cap, n_c = sizes
    half = cap // 2
    low = half + 8
    n_feat, n_tok = tok_ref.shape
    edge = n_feat - LANES
    width = n_feat * n_e
    wide = width // n_c
    per = n_e // n_c
    rows = N_X * cap
    sec = lax.axis_index("section")
    z = lax.axis_index("expert")
    d = lax.axis_index("dp")
    xh = lax.div(sec, n_y)
    y = lax.rem(sec, n_y)
    up = xh * n_y + lax.rem(y + 1, n_y)
    down = xh * n_y + lax.rem(y + n_y - 1, n_y)
    across = (1 - xh) * n_y + y
    other = 1 - xh
    chip = lax.div(d, 2)
    core = lax.rem(d, 2)
    mine = lax.div(z, per)
    spread = sorted(range(n_c), key=lambda i: min(i, n_c - i))
    near_first = [lax.rem(mine + i, n_c) for i in spread]
    far_first = near_first[::-1]

    def ring(h):
        return xh * n_y + lax.rem(y + 1 + h * (n_y - 2), n_y)

    def remote(src, dst, send, recv, **where):
        return pltpu.make_async_remote_copy(
            src_ref=src,
            dst_ref=dst,
            send_sem=send,
            recv_sem=recv,
            device_id=where,
            device_id_type=pl.DeviceIdType.MESH,
        )

    barrier = pltpu.get_barrier_semaphore()

    def greet(**where):
        pl.semaphore_signal(barrier, inc=1, device_id=where, device_id_type=pl.DeviceIdType.MESH)

    order = sorted(range(1, n_e), key=lambda i: -min(i, n_e - i))
    for i in order:
        greet(expert=lax.rem(z + i, n_e))
    for to in (across, up, down):
        greet(section=to)
    for i in range(1, n_d):
        greet(dp=lax.rem(d + i, n_d))

    small = [
        pltpu.make_async_copy(src, dst, w_sem.at[i])
        for i, (src, dst) in enumerate(
            ((routes_hbm, routes_ref), (gates_hbm, gates_ref), (tok_hbm, tok_ref), (gain_hbm, gain_ref))
        )
    ]
    loads = [
        pltpu.make_async_copy(src.at[0], dst, w_sem.at[4 + i])
        for i, (src, dst) in enumerate(((wg_hbm, wg), (wu_hbm, wu), (wd_hbm, wd)))
    ]
    for load in small + loads:
        load.start()
    for load in small:
        load.wait()

    first = routes_ref[0:1, :]
    second = routes_ref[1:2, :]
    expert_ids = lax.broadcasted_iota(jnp.int32, (n_e, n_tok), 0)
    named = (first == expert_ids) | (second == expert_ids)
    earlier = (
        lax.broadcasted_iota(jnp.int32, (n_tok, n_tok), 0) < lax.broadcasted_iota(jnp.int32, (n_tok, n_tok), 1)
    )
    count = dot(jnp.where(named, 1.0, 0.0).astype(BF16), jnp.where(earlier, 1.0, 0.0).astype(BF16))
    slot = jnp.where(named, count, -1.0)
    weight = jnp.where(first == expert_ids, gates_ref[0:1, :], gates_ref[1:2, :])
    number = lax.broadcasted_iota(jnp.int32, (cap, n_tok), 0).astype(F32)
    picks = [jnp.where(slot[e : e + 1, :] == number, 1.0, 0.0) for e in range(n_e)]
    eye = lax.broadcasted_iota(jnp.int32, (cap, LANES), 0) == lax.broadcasted_iota(jnp.int32, (cap, LANES), 1)
    picked = dot_last(jnp.concatenate([p.astype(BF16) for p in picks], axis=0), tok_ref[...])
    squares = jnp.sum(picked * picked, axis=1, keepdims=True)
    picked = picked * gain_ref[...]
    for e in range(n_e):
        top, below = pack(picked[e * cap : (e + 1) * cap])
        go[e, 0:cap, :] = top.astype(BF16)
        terms = split3(jnp.sum(jnp.where(eye, squares[e * cap : (e + 1) * cap], 0.0), axis=0, keepdims=True))
        go[e, cap : cap + low, :] = jnp.concatenate(
            [below] + list(terms) + [jnp.zeros((5, LANES), F32)], axis=0
        ).astype(BF16)

    pl.semaphore_wait(barrier, n_e - 1 + n_d - 1 + 3)

    def z_copy(src, dst, send, recv, to):
        return remote(src.at[to], dst.at[z], send, recv, expert=to)

    for i in order:
        z_copy(go, got, go_s, go_r.at[z], lax.rem(z + i, n_e)).start()
    got[z] = go[z]

    def x_copy(c):
        return remote(ag.at[0, xh, c], ag.at[0, xh, c], x_s, x_r.at[c], section=across)

    def ag_copy(b, h, c):
        at = lax.rem(b, RING)
        return remote(
            ag.at[b, h, c], ag.at[b + 1, h, c], ag_s.at[at, h], ag_r.at[lax.rem(b + 1, RING), h, c], section=ring(h)
        )

    def ag_sent(b, h):
        remote(ag.at[b, h], ag.at[b, h], ag_s.at[lax.rem(b, RING), h], ag_r.at[0, h, 0], section=ring(h)).wait_send()

    def ag_wait(b, h, c):
        at = lax.rem(b, RING)
        remote(ag.at[b, h, c], ag.at[b, h, c], ag_s.at[at, h], ag_r.at[at, h, c], section=ring(h)).wait_recv()

    def ag_cross(c):
        return remote(ag.at[n_y - 1, xh, c], ag.at[n_y - 1, xh, c], ax_s, ax_r, section=across)

    low_row = lax.broadcasted_iota(jnp.int32, (low, n_tok), 0)
    low_number = jnp.where(low_row < half, low_row, 4 * cap).astype(F32)
    for e in range(n_e):
        mark = slot[e : e + 1, :]
        w = weight[e : e + 1, :]
        for part, store, lead, size in (
            (picks[e], mix_top, 0, cap),
            (jnp.where(mark == low_number, 1.0, 0.0), mix_low, 0, low),
            (jnp.where(mark == low_number + half, 1.0, 0.0), mix_low, 2, low),
        ):
            value = part * w
            high = value.astype(BF16)
            store[lead, e * size : (e + 1) * size, :] = high
            store[lead + 1, e * size : (e + 1) * size, :] = (value - high.astype(F32)).astype(BF16)

    row_squares = jnp.zeros((1, LANES), F32)
    for c in near_first:
        pieces = []
        for k in range(per):
            zp = c * per + k

            @pl.when(zp != z)
            def _():
                remote(go.at[zp], got.at[zp], go_s, go_r.at[zp], expert=zp).wait_recv()

            block = got[zp].astype(F32)
            below = block[cap : cap + half]
            pieces.append(
                jnp.concatenate(
                    [block[:cap], jnp.concatenate([below[:, :edge], below[:, edge : 2 * edge]], axis=0)], axis=1
                )
            )
            terms = block[cap + half : cap + half + 8]
            row_squares = row_squares + (terms[0:1] + terms[1:2] + terms[2:3])
        ag[0, xh, c] = jnp.concatenate(pieces, axis=1).astype(BF16)
        x_copy(c).start()
        ag_copy(0, xh, c).start()

    def d_copy(src, dst, send, recv, i):
        return remote(src, dst.at[i - 1], send, recv, dp=lax.rem(d + i, n_d))

    def d_all(dst, send, recv):
        return remote(dst, dst, send, recv, dp=lax.rem(d + 1, n_d))

    ss_out[...] = jnp.broadcast_to(row_squares, ss_out.shape)
    for i in range(1, n_d):
        d_copy(ss_out, ss_in, ss_s, ss_r, i).start()
    for c in near_first:
        ag_wait(1, xh, c)
        ag_copy(1, xh, c).start()
        remote(ag.at[0, other, c], ag.at[0, other, c], x_s, x_r.at[c], section=across).wait_recv()
        ag_copy(0, other, c).start()
    d_all(ss_in, ss_s, ss_r).wait_recv()
    total = row_squares
    for i in range(n_d - 1):
        total = total + ss_in[i][0:1, :]
    sc[0, xh] = jnp.broadcast_to(lax.rsqrt(total / (n_d * width) + EPS), ss_out.shape)
    sx_copy = remote(sc.at[0, xh], sc.at[0, xh], sx_s, sx_r, section=across)
    sx_copy.start()
    for load in loads:
        load.wait()

    def sc_copy(b, h):
        at = lax.rem(b, 2)
        return remote(sc.at[b, h], sc.at[b + 1, h], sc_s.at[at, h], sc_r.at[1 - at, h], section=ring(h))

    def core_copy(b):
        at = lax.rem(b, 2)
        return remote(part_out.at[b, 1 - core], core_in.at[b], core_s.at[at], core_r.at[at], dp=2 * chip + 1 - core)

    def pair_copy(b):
        at = lax.rem(b, TURN)
        return remote(pair_out.at[b], pair_in.at[b], pair_s.at[at], pair_r.at[at], dp=2 * (1 - chip) + core)

    def hid_copy(b, which):
        at = lax.rem(b, TURN)
        return remote(hid.at[b, which], hid.at[b, which], hid_s.at[at], hid_r.at[at], dp=2 * chip + 1 - core)

    def rs_copy(b, h, c):
        return remote(
            rs_out.at[b, h, c],
            rs_in.at[b + 1, h, c],
            rs_s.at[lax.rem(b, RING), h],
            rs_r.at[lax.rem(b + 1, RING), h, c],
            section=ring(h),
        )

    def rs_wait(b, h, c):
        at = lax.rem(b, RING)
        remote(rs_in.at[b, h, c], rs_in.at[b, h, c], rs_s.at[at, h], rs_r.at[at, h, c], section=ring(h)).wait_recv()

    def rs_sent(b, h):
        some = rs_out.at[b, h]
        remote(some, some, rs_s.at[lax.rem(b, RING), h], rs_r.at[0, h, 0], section=ring(h)).wait_send()

    unit = wg.shape[1] // 2

    def gate_up(b):
        @pl.when(b > 1)
        def _():
            core_copy(b - 2).wait_send()

        @pl.when(b == n_y - 1)
        def _():
            last = ag.at[n_y - 1, other]
            remote(last, last, ax_s, ax_r, section=across).wait_recv()

        block = jnp.concatenate([ag[b, :, c].reshape(rows, wide) for c in range(n_c)], axis=1)
        gate = dot(block, wg[...]).astype(BF16)
        upper = dot(block, wu[...]).astype(BF16)
        for p in range(2):
            part_out[b, p, :, 0:unit] = gate[:, p * unit : (p + 1) * unit]
            part_out[b, p, :, unit : 2 * unit] = upper[:, p * unit : (p + 1) * unit]
        core_copy(b).start()

    def chip_sum(b):
        @pl.when(b >= TURN)
        def _():
            pair_copy(b - TURN).wait_send()

        core_copy(b).wait_recv()
        pair_out[b] = (part_out[b, core].astype(F32) + core_in[b].astype(F32)).astype(BF16)
        pair_copy(b).start()

    def hidden_units(b):
        @pl.when(b == 0)
        def _():
            remote(sc.at[0, 1 - xh], sc.at[0, 1 - xh], sx_s, sx_r, section=across).wait_recv()

        @pl.when(b > 0)
        def _():
            for h in range(N_X):
                remote(
                    sc.at[b, h], sc.at[b, h], sc_s.at[0, h], sc_r.at[lax.rem(b, 2), h], section=ring(h)
                ).wait_recv()

        @pl.when((b > 1) & (b < n_y - 1))
        def _():
            for h in range(N_X):
                sc_copy(b - 2, h).wait_send()

        @pl.when(b < n_y - 1)
        def _():
            for h in range(N_X):
                sc_copy(b, h).start()

        @pl.when(b >= TURN)
        def _():
            hid_copy(b - TURN, core).wait_send()

        scales = [jnp.sum(jnp.where(eye, sc[b, h][0:1, :], 0.0), axis=1, keepdims=True) for h in range(N_X)]
        pair_copy(b).wait_recv()
        both = part_out[b, core].astype(F32) + core_in[b].astype(F32) + pair_in[b].astype(F32)
        both = both * jnp.concatenate(scales, axis=0)
        g = both[:, 0:unit]
        hid[b, core] = (g / (1.0 + jnp.exp(-g)) * both[:, unit : 2 * unit]).astype(BF16)
        hid_copy(b, core).start()

    def down_product(b):
        hid_copy(b, 1 - core).wait_recv()
        result = dot(jnp.concatenate([hid[b, 0], hid[b, 1]], axis=1), wd[...])

        def keep(ref):
            for h in range(N_X):
                for c in range(n_c):
                    ref[h, c] = result[h * cap : (h + 1) * cap, c * wide : (c + 1) * wide]

        @pl.when(b == 0)
        def _():
            keep(own)

        @pl.when(b > 0)
        def _():
            keep(res.at[lax.rem(b, 2)])

        @pl.when(b == 1)
        def _():
            for c in far_first:
                cross_out[c] = res[1, other, c].astype(BF16)
                rs_cross(c).start()

    def rs_cross(c):
        return remote(cross_out.at[c], cross_in.at[c], rx_s, rx_r.at[c], section=across)

    def xr_copy(c):
        return remote(xr_out.at[c], xr_in.at[c], xr_s, xr_r.at[c], section=across)

    def add_own(b, c):
        mine = res[lax.rem(b, 2), xh, c]

        @pl.when(b == 1)
        def _():
            rs_cross(c).wait_recv()
            rs_out[b, xh, c] = (mine + cross_in[c].astype(F32)).astype(BF16)

        @pl.when(b > 1)
        def _():
            rs_wait(b, xh, c)
            rs_out[b, xh, c] = (mine + rs_in[b, xh, c].astype(F32)).astype(BF16)

        rs_copy(b, xh, c).start()

    def add_other(b, c):
        @pl.when(b < n_y)
        def _():
            mine = res[lax.rem(b, 2), other, c]

            @pl.when(b == 2)
            def _():
                rs_out[b, other, c] = mine.astype(BF16)

            @pl.when(b > 2)
            def _():
                rs_wait(b, other, c)
                rs_out[b, other, c] = (mine + rs_in[b, other, c].astype(F32)).astype(BF16)

            rs_copy(b, other, c).start()

        @pl.when(b == n_y)
        def _():
            rs_wait(n_y, other, c)
            xr_out[c] = (own[other, c] + rs_in[n_y, other, c].astype(F32)).astype(BF16)
            xr_copy(c).start()

    def add_on(t, c):
        @pl.when((t > 3) & (t < n_y + 3))
        def _():
            add_own(t - 3, c)
            add_other(t - 2, c)

    def step(t, carry):
        @pl.when(t <= n_y)
        def _():
            gate_up(t - 1)

        @pl.when((t > 1) & (t < n_y - 2))
        def _():
            ag_sent(t - 2, xh)

        @pl.when((t >= RING) & (t < n_y - 2))
        def _():
            ag_sent(t - RING, other)

        for j in range(n_c):
            c = near_first[j]

            @pl.when(t < n_y - 1)
            def _():
                ag_wait(t + 1, xh, c)

                @pl.when(t < n_y - 2)
                def _():
                    ag_copy(t + 1, xh, c).start()

                @pl.when(t == n_y - 2)
                def _():
                    ag_cross(c).start()

                ag_wait(t, other, c)

                @pl.when(t < n_y - 2)
                def _():
                    ag_copy(t, other, c).start()

            if j == min(PAIR_AT, n_c - 1):

                @pl.when(t <= n_y)
                def _():
                    chip_sum(t - 1)

            if j == min(HIDDEN_AT, n_c - 1):

                @pl.when((t > 1) & (t < n_y + 2))
                def _():
                    hidden_units(t - 2)

            if j == down_at:

                @pl.when((t > 1) & (t < n_y + 2))
                def _():
                    down_product(t - 2)

                @pl.when((t > 3 + RING) & (t < n_y + 3))
                def _():
                    rs_sent(t - 3 - RING, xh)

                @pl.when((t > 3 + RING) & (t < n_y + 2))
                def _():
                    rs_sent(t - 2 - RING, other)

            if j >= down_at:
                add_on(t, far_first[j - down_at])
            else:
                add_on(t - 1, far_first[j - down_at + n_c])

        return carry

    down_at = min(DOWN_AT, n_c - 1)
    lax.fori_loop(1, n_y + 4, step, 0)

    for c in far_first:
        xr_copy(c).wait_recv()
        answer = own[xh, c] + xr_in[c].astype(F32)
        rs_wait(n_y, xh, c)
        answer = answer + rs_in[n_y, xh, c].astype(F32)
        for k in range(per):
            zp = c * per + k
            top, below = pack(answer[:, k * n_feat : (k + 1) * n_feat])
            bk_out[zp, 0:cap, :] = top.astype(BF16)
            bk_out[zp, cap : cap + low, :] = jnp.concatenate([below, jnp.zeros((8, LANES), F32)], axis=0).astype(BF16)

            @pl.when(zp != z)
            def _():
                z_copy(bk_out, bk_in, bk_s, bk_r, zp).start()

    bk_in[z] = bk_out[z]

    def z_all(src, send, recv):
        some = src.at[pl.ds(0, n_e - 1)]
        return remote(some, some, send, recv, expert=lax.rem(z + 1, n_e))

    z_all(bk_in, bk_s, bk_r).wait_recv()
    back_top = bk_in[:, 0:cap, :].reshape(n_e * cap, LANES)
    back_low = bk_in[:, cap : cap + low, :].reshape(n_e * low, LANES)
    out_ref[0:LANES, :] = (
        tok_ref[0:LANES, :].astype(F32) + dot_first(back_top, mix_top[0]) + dot_first(back_top, mix_top[1])
    ).astype(BF16)
    low_a = dot_first(back_low, mix_low[0]) + dot_first(back_low, mix_low[1])
    low_b = dot_first(back_low, mix_low[2]) + dot_first(back_low, mix_low[3])
    out_ref[LANES:n_feat, :] = (
        tok_ref[LANES:n_feat, :].astype(F32) + low_a[0:edge] + low_b[edge : 2 * edge]
    ).astype(BF16)

    z_all(go, go_s, go_r.at[0]).wait_send()
    z_all(bk_out, bk_s, bk_r).wait_send()
    d_all(ss_in, ss_s, ss_r).wait_send()
    sx_copy.wait_send()
    remote(ag.at[0, xh], ag.at[0, xh], x_s, x_r.at[0], section=across).wait_send()
    remote(xr_out, xr_out, xr_s, xr_r.at[0], section=across).wait_send()
    for h in range(N_X):
        for b in range(max(0, n_y - 3), n_y - 1):
            sc_copy(b, h).wait_send()
    for b in range(max(0, n_y - 1 - RING), n_y - 1):
        ag_sent(b, xh)
    for b in range(max(0, n_y - 2 - RING), n_y - 2):
        ag_sent(b, other)
    for b in range(max(1, n_y - RING), n_y):
        rs_sent(b, xh)
    for b in range(max(2, n_y - RING), n_y):
        rs_sent(b, other)
    remote(ag.at[n_y - 1, xh], ag.at[n_y - 1, xh], ax_s, ax_r, section=across).wait_send()
    remote(cross_out, cross_out, rx_s, rx_r.at[0], section=across).wait_send()
    for b in range(n_y - 2, n_y):
        core_copy(b).wait_send()
    for b in range(max(0, n_y - TURN), n_y):
        pair_copy(b).wait_send()
        hid_copy(b, core).wait_send()


def local(tokens, norm_gain, routes, gates, w_gate, w_up, w_down):
    n_tok, n_feat = tokens.shape
    n_e = lax.axis_size("expert")
    n_d = lax.axis_size("dp")
    n_y = lax.axis_size("section") // N_X
    n_c = min(CHUNKS, n_e)
    cap = min(n_tok, max(2, 3 * n_tok // n_e))
    low = cap // 2 + 8
    width = n_feat * n_e
    wide = width // n_c
    units = w_gate.shape[2]
    unit = units // 2
    rows = N_X * cap
    dma = pltpu.SemaphoreType.DMA
    far = pl.BlockSpec(memory_space=pl.ANY)
    scratch = [
        pltpu.VMEM((n_feat, n_tok), BF16),
        pltpu.VMEM((1, n_feat), F32),
        pltpu.VMEM((2, n_tok), jnp.int32),
        pltpu.VMEM((2, n_tok), F32),
        pltpu.VMEM((width, units), BF16),
        pltpu.VMEM((width, units), BF16),
        pltpu.VMEM((units, width), BF16),
        dma((7,)),
        pltpu.VMEM((2, n_e * cap, n_tok), BF16),
        pltpu.VMEM((4, n_e * low, n_tok), BF16),
        pltpu.VMEM((n_e, cap + low, LANES), BF16),
        pltpu.VMEM((n_e, cap + low, LANES), BF16),
        pltpu.VMEM((8, LANES), F32),
        pltpu.VMEM((n_d - 1, 8, LANES), F32),
        pltpu.VMEM((n_y, N_X, 8, LANES), F32),
        pltpu.VMEM((n_y, N_X, n_c, cap, wide), BF16),
        pltpu.VMEM((n_y, 2, rows, 2 * unit), BF16),
        pltpu.VMEM((n_y, rows, 2 * unit), BF16),
        pltpu.VMEM((n_y, rows, 2 * unit), BF16),
        pltpu.VMEM((n_y, rows, 2 * unit), BF16),
        pltpu.VMEM((n_y, 2, rows, unit), BF16),
        pltpu.VMEM((N_X, n_c, cap, wide), F32),
        pltpu.VMEM((2, N_X, n_c, cap, wide), F32),
        pltpu.VMEM((n_c, cap, wide), BF16),
        pltpu.VMEM((n_c, cap, wide), BF16),
        pltpu.VMEM((n_y, N_X, n_c, cap, wide), BF16),
        pltpu.VMEM((n_y + 1, N_X, n_c, cap, wide), BF16),
        pltpu.VMEM((n_c, cap, wide), BF16),
        pltpu.VMEM((n_c, cap, wide), BF16),
        pltpu.VMEM((n_e, cap + low, LANES), BF16),
        pltpu.VMEM((n_e, cap + low, LANES), BF16),
        dma,
        dma((n_e,)),
        dma,
        dma,
        dma,
        dma,
        dma((2, N_X)),
        dma((2, N_X)),
        dma,
        dma((n_c,)),
        dma((RING, N_X)),
        dma((RING, N_X, n_c)),
        dma,
        dma,
        dma((2,)),
        dma((2,)),
        dma((TURN,)),
        dma((TURN,)),
        dma((TURN,)),
        dma((TURN,)),
        dma((RING, N_X)),
        dma((RING, N_X, n_c)),
        dma,
        dma((n_c,)),
        dma,
        dma((n_c,)),
        dma,
        dma,
    ]
    mixed = pl.pallas_call(
        functools.partial(kernel, (n_y, n_e, n_d, cap, n_c)),
        out_shape=jax.ShapeDtypeStruct((n_feat, n_tok), BF16),
        in_specs=[far] * 7,
        out_specs=pl.BlockSpec(memory_space=pltpu.VMEM),
        scratch_shapes=scratch,
        compiler_params=pltpu.CompilerParams(
            collective_id=0, has_side_effects=True, vmem_limit_bytes=64 * 1024 * 1024
        ),
        name="moe_layer",
    )(tokens.T, norm_gain.reshape(1, n_feat), routes.T, gates.T, w_gate, w_up, w_down)
    return mixed.T


def solution(mesh):
    in_specs = (
        P("section", ("dp", "expert")),
        P(("dp", "expert")),
        P("section", None),
        P("section", None),
        P("expert", "dp", "section"),
        P("expert", "dp", "section"),
        P("expert", "section", "dp"),
    )
    out_specs = P("section", ("dp", "expert"))
    return jax.shard_map(local, mesh=mesh, in_specs=in_specs, out_specs=out_specs, check_vma=False)
```

```python
import functools

import jax
import jax.numpy as jnp
from jax import lax
from jax.experimental import pallas as pl
from jax.experimental.pallas import tpu as pltpu
from jax.sharding import PartitionSpec as P

D = 6144
EPS = 1e-05
N_X = 2
F32 = jnp.float32
BF16 = jnp.bfloat16
LANES = 128
CHUNKS = 4
RING = 3
TURN = 4
PAIR_AT, HIDDEN_AT, DOWN_AT = 1, 3, 4


def dot(a, b):
    return jnp.dot(a, b, preferred_element_type=F32)


def dot_last(a, b):
    return lax.dot_general(a, b, (((1,), (1,)), ((), ())), preferred_element_type=F32)


def dot_first(a, b):
    return lax.dot_general(a, b, (((0,), (0,)), ((), ())), preferred_element_type=F32)


def split3(v):
    high = v.astype(BF16).astype(F32)
    rest = v - high
    mid = rest.astype(BF16).astype(F32)
    return high, mid, rest - mid


def pack(rows):
    half = rows.shape[0] // 2
    tail = rows[:, LANES:]
    return rows[:, :LANES], jnp.concatenate([tail[:half], tail[half:]], axis=1)


def kernel(
    sizes,
    tok_hbm,
    gain_hbm,
    routes_hbm,
    gates_hbm,
    wg_hbm,
    wu_hbm,
    wd_hbm,
    out_ref,
    tok_ref,
    gain_ref,
    routes_ref,
    gates_ref,
    wg,
    wu,
    wd,
    w_sem,
    mix_top,
    mix_low,
    go,
    got,
    ss_out,
    ss_in,
    sc,
    ag,
    part_out,
    core_in,
    pair_out,
    pair_in,
    hid,
    own,
    res,
    cross_out,
    cross_in,
    straight_out,
    straight_in,
    rs_out,
    rs_in,
    xr_out,
    xr_in,
    bk_out,
    bk_in,
    go_s,
    go_r,
    ss_s,
    ss_r,
    sx_s,
    sx_r,
    sc_s,
    sc_r,
    x_s,
    x_r,
    ag_s,
    ag_r,
    dr_s,
    dr_r,
    ax_s,
    ax_r,
    core_s,
    core_r,
    pair_s,
    pair_r,
    hid_s,
    hid_r,
    rs_s,
    rs_r,
    rx_s,
    rx_r,
    dt_s,
    dt_r,
    xr_s,
    xr_r,
    bk_s,
    bk_r,
):
    n_y, n_e, n_d, cap, n_c = sizes
    half = cap // 2
    low = half + 8
    n_feat, n_tok = tok_ref.shape
    edge = n_feat - LANES
    width = n_feat * n_e
    wide = width // n_c
    per = n_e // n_c
    rows = N_X * cap
    sec = lax.axis_index("section")
    z = lax.axis_index("expert")
    d = lax.axis_index("dp")
    xh = lax.div(sec, n_y)
    y = lax.rem(sec, n_y)
    up = xh * n_y + lax.rem(y + 1, n_y)
    down = xh * n_y + lax.rem(y + n_y - 1, n_y)
    across = (1 - xh) * n_y + y
    other = 1 - xh
    chip = lax.div(d, 2)
    core = lax.rem(d, 2)
    mine = lax.div(z, per)
    spread = sorted(range(n_c), key=lambda i: min(i, n_c - i))
    near_first = [lax.rem(mine + i, n_c) for i in spread]
    far_first = near_first[::-1]

    def ring(h):
        return xh * n_y + lax.rem(y + 1 + h * (n_y - 2), n_y)

    def remote(src, dst, send, recv, **where):
        return pltpu.make_async_remote_copy(
            src_ref=src,
            dst_ref=dst,
            send_sem=send,
            recv_sem=recv,
            device_id=where,
            device_id_type=pl.DeviceIdType.MESH,
        )

    barrier = pltpu.get_barrier_semaphore()

    def greet(**where):
        pl.semaphore_signal(barrier, inc=1, device_id=where, device_id_type=pl.DeviceIdType.MESH)

    order = sorted(range(1, n_e), key=lambda i: -min(i, n_e - i))
    for i in order:
        greet(expert=lax.rem(z + i, n_e))
    for to in (across, up, down):
        greet(section=to)
    for i in range(1, n_d):
        greet(dp=lax.rem(d + i, n_d))

    small = [
        pltpu.make_async_copy(src, dst, w_sem.at[i])
        for i, (src, dst) in enumerate(
            ((routes_hbm, routes_ref), (gates_hbm, gates_ref), (tok_hbm, tok_ref), (gain_hbm, gain_ref))
        )
    ]
    loads = [
        pltpu.make_async_copy(src.at[0], dst, w_sem.at[4 + i])
        for i, (src, dst) in enumerate(((wg_hbm, wg), (wu_hbm, wu), (wd_hbm, wd)))
    ]
    for load in small + loads:
        load.start()
    for load in small:
        load.wait()

    first = routes_ref[0:1, :]
    second = routes_ref[1:2, :]
    expert_ids = lax.broadcasted_iota(jnp.int32, (n_e, n_tok), 0)
    named = (first == expert_ids) | (second == expert_ids)
    earlier = (
        lax.broadcasted_iota(jnp.int32, (n_tok, n_tok), 0) < lax.broadcasted_iota(jnp.int32, (n_tok, n_tok), 1)
    )
    count = dot(jnp.where(named, 1.0, 0.0).astype(BF16), jnp.where(earlier, 1.0, 0.0).astype(BF16))
    slot = jnp.where(named, count, -1.0)
    weight = jnp.where(first == expert_ids, gates_ref[0:1, :], gates_ref[1:2, :])
    number = lax.broadcasted_iota(jnp.int32, (cap, n_tok), 0).astype(F32)
    picks = [jnp.where(slot[e : e + 1, :] == number, 1.0, 0.0) for e in range(n_e)]
    eye = lax.broadcasted_iota(jnp.int32, (cap, LANES), 0) == lax.broadcasted_iota(jnp.int32, (cap, LANES), 1)
    picked = dot_last(jnp.concatenate([p.astype(BF16) for p in picks], axis=0), tok_ref[...])
    squares = jnp.sum(picked * picked, axis=1, keepdims=True)
    picked = picked * gain_ref[...]
    for e in range(n_e):
        top, below = pack(picked[e * cap : (e + 1) * cap])
        go[e, 0:cap, :] = top.astype(BF16)
        terms = split3(jnp.sum(jnp.where(eye, squares[e * cap : (e + 1) * cap], 0.0), axis=0, keepdims=True))
        go[e, cap : cap + low, :] = jnp.concatenate(
            [below] + list(terms) + [jnp.zeros((5, LANES), F32)], axis=0
        ).astype(BF16)

    pl.semaphore_wait(barrier, n_e - 1 + n_d - 1 + 3)

    def z_copy(src, dst, send, recv, to):
        return remote(src.at[to], dst.at[z], send, recv, expert=to)

    for i in order[::-1]:
        z_copy(go, got, go_s, go_r.at[z], lax.rem(z + i, n_e)).start()
    got[z] = go[z]

    def x_copy(c):
        return remote(ag.at[0, xh, c], ag.at[0, xh, c], x_s, x_r.at[c], section=across)

    def ag_copy(b, h, c):
        at = lax.rem(b, RING)
        return remote(
            ag.at[b, h, c], ag.at[b + 1, h, c], ag_s.at[at, h], ag_r.at[lax.rem(b + 1, RING), h, c], section=ring(h)
        )

    def ag_sent(b, h):
        remote(ag.at[b, h], ag.at[b, h], ag_s.at[lax.rem(b, RING), h], ag_r.at[0, h, 0], section=ring(h)).wait_send()

    def ag_wait(b, h, c):
        at = lax.rem(b, RING)
        remote(ag.at[b, h, c], ag.at[b, h, c], ag_s.at[at, h], ag_r.at[at, h, c], section=ring(h)).wait_recv()

    def ag_straight(c):
        return remote(ag.at[0, xh, c], ag.at[n_y - 1, xh, c], dr_s, dr_r, section=ring(other))

    def ag_last(send, recv, **where):
        return remote(ag.at[n_y - 1, xh], ag.at[n_y - 1, xh], send, recv, **where)

    low_row = lax.broadcasted_iota(jnp.int32, (low, n_tok), 0)
    low_number = jnp.where(low_row < half, low_row, 4 * cap).astype(F32)
    for e in range(n_e):
        mark = slot[e : e + 1, :]
        w = weight[e : e + 1, :]
        for part, store, lead, size in (
            (picks[e], mix_top, 0, cap),
            (jnp.where(mark == low_number, 1.0, 0.0), mix_low, 0, low),
            (jnp.where(mark == low_number + half, 1.0, 0.0), mix_low, 2, low),
        ):
            value = part * w
            high = value.astype(BF16)
            store[lead, e * size : (e + 1) * size, :] = high
            store[lead + 1, e * size : (e + 1) * size, :] = (value - high.astype(F32)).astype(BF16)

    row_squares = jnp.zeros((1, LANES), F32)
    for c in near_first:
        pieces = []
        for k in range(per):
            zp = c * per + k

            @pl.when(zp != z)
            def _():
                remote(go.at[zp], got.at[zp], go_s, go_r.at[zp], expert=zp).wait_recv()

            block = got[zp].astype(F32)
            below = block[cap : cap + half]
            pieces.append(
                jnp.concatenate(
                    [block[:cap], jnp.concatenate([below[:, :edge], below[:, edge : 2 * edge]], axis=0)], axis=1
                )
            )
            terms = block[cap + half : cap + half + 8]
            row_squares = row_squares + (terms[0:1] + terms[1:2] + terms[2:3])
        ag[0, xh, c] = jnp.concatenate(pieces, axis=1).astype(BF16)
        x_copy(c).start()
        ag_copy(0, xh, c).start()
        ag_straight(c).start()

    def d_copy(src, dst, send, recv, i):
        return remote(src, dst.at[i - 1], send, recv, dp=lax.rem(d + i, n_d))

    def d_all(dst, send, recv):
        return remote(dst, dst, send, recv, dp=lax.rem(d + 1, n_d))

    ss_out[...] = jnp.broadcast_to(row_squares, ss_out.shape)
    for i in range(1, n_d):
        d_copy(ss_out, ss_in, ss_s, ss_r, i).start()
    for c in near_first:
        ag_wait(1, xh, c)
        ag_copy(1, xh, c).start()
        remote(ag.at[0, other, c], ag.at[0, other, c], x_s, x_r.at[c], section=across).wait_recv()
        ag_copy(0, other, c).start()
    d_all(ss_in, ss_s, ss_r).wait_recv()
    total = row_squares
    for i in range(n_d - 1):
        total = total + ss_in[i][0:1, :]
    sc[0, xh] = jnp.broadcast_to(lax.rsqrt(total / (n_d * width) + EPS), ss_out.shape)
    sx_copy = remote(sc.at[0, xh], sc.at[0, xh], sx_s, sx_r, section=across)
    sx_copy.start()
    for load in loads:
        load.wait()

    def sc_copy(b, h):
        at = lax.rem(b, 2)
        return remote(sc.at[b, h], sc.at[b + 1, h], sc_s.at[at, h], sc_r.at[1 - at, h], section=ring(h))

    def core_copy(b):
        at = lax.rem(b, 2)
        return remote(part_out.at[b, 1 - core], core_in.at[b], core_s.at[at], core_r.at[at], dp=2 * chip + 1 - core)

    def pair_copy(b):
        at = lax.rem(b, TURN)
        return remote(pair_out.at[b], pair_in.at[b], pair_s.at[at], pair_r.at[at], dp=2 * (1 - chip) + core)

    def hid_copy(b, which):
        at = lax.rem(b, TURN)
        return remote(hid.at[b, which], hid.at[b, which], hid_s.at[at], hid_r.at[at], dp=2 * chip + 1 - core)

    def rs_copy(b, h, c):
        return remote(
            rs_out.at[b, h, c],
            rs_in.at[b + 1, h, c],
            rs_s.at[lax.rem(b, RING), h],
            rs_r.at[lax.rem(b + 1, RING), h, c],
            section=ring(h),
        )

    def rs_wait(b, h, c):
        at = lax.rem(b, RING)
        remote(rs_in.at[b, h, c], rs_in.at[b, h, c], rs_s.at[at, h], rs_r.at[at, h, c], section=ring(h)).wait_recv()

    def rs_sent(b, h):
        some = rs_out.at[b, h]
        remote(some, some, rs_s.at[lax.rem(b, RING), h], rs_r.at[0, h, 0], section=ring(h)).wait_send()

    unit = wg.shape[1] // 2

    def gate_up(b):
        @pl.when(b > 1)
        def _():
            core_copy(b - 2).wait_send()

        @pl.when(b == n_y - 1)
        def _():
            last = ag.at[n_y - 1, other]
            remote(last, last, ax_s, ax_r, section=across).wait_recv()

        block = jnp.concatenate([ag[b, :, c].reshape(rows, wide) for c in range(n_c)], axis=1)
        gate = dot(block, wg[...]).astype(BF16)
        upper = dot(block, wu[...]).astype(BF16)
        for p in range(2):
            part_out[b, p, :, 0:unit] = gate[:, p * unit : (p + 1) * unit]
            part_out[b, p, :, unit : 2 * unit] = upper[:, p * unit : (p + 1) * unit]
        core_copy(b).start()

    def chip_sum(b):
        @pl.when(b >= TURN)
        def _():
            pair_copy(b - TURN).wait_send()

        core_copy(b).wait_recv()
        pair_out[b] = (part_out[b, core].astype(F32) + core_in[b].astype(F32)).astype(BF16)
        pair_copy(b).start()

    def hidden_units(b):
        @pl.when(b == 0)
        def _():
            remote(sc.at[0, 1 - xh], sc.at[0, 1 - xh], sx_s, sx_r, section=across).wait_recv()

        @pl.when(b > 0)
        def _():
            for h in range(N_X):
                remote(
                    sc.at[b, h], sc.at[b, h], sc_s.at[0, h], sc_r.at[lax.rem(b, 2), h], section=ring(h)
                ).wait_recv()

        @pl.when((b > 1) & (b < n_y - 1))
        def _():
            for h in range(N_X):
                sc_copy(b - 2, h).wait_send()

        @pl.when(b < n_y - 1)
        def _():
            for h in range(N_X):
                sc_copy(b, h).start()

        @pl.when(b >= TURN)
        def _():
            hid_copy(b - TURN, core).wait_send()

        scales = [jnp.sum(jnp.where(eye, sc[b, h][0:1, :], 0.0), axis=1, keepdims=True) for h in range(N_X)]
        pair_copy(b).wait_recv()
        both = part_out[b, core].astype(F32) + core_in[b].astype(F32) + pair_in[b].astype(F32)
        both = both * jnp.concatenate(scales, axis=0)
        g = both[:, 0:unit]
        hid[b, core] = (g / (1.0 + jnp.exp(-g)) * both[:, unit : 2 * unit]).astype(BF16)
        hid_copy(b, core).start()

    def down_product(b):
        hid_copy(b, 1 - core).wait_recv()
        result = dot(jnp.concatenate([hid[b, 0], hid[b, 1]], axis=1), wd[...])

        def keep(ref):
            for h in range(N_X):
                for c in range(n_c):
                    ref[h, c] = result[h * cap : (h + 1) * cap, c * wide : (c + 1) * wide]

        @pl.when(b == 0)
        def _():
            keep(own)

        @pl.when(b > 0)
        def _():
            keep(res.at[lax.rem(b, 2)])

        @pl.when(b == 1)
        def _():
            for c in far_first:
                cross_out[c] = res[1, other, c].astype(BF16)
                rs_cross(c).start()

    def rs_cross(c):
        return remote(cross_out.at[c], cross_in.at[c], rx_s, rx_r.at[c], section=across)

    def xr_copy(c):
        return remote(xr_out.at[c], xr_in.at[c], xr_s, xr_r.at[c], section=across)

    def straight_copy(c):
        return remote(straight_out.at[c], straight_in.at[c], dt_s, dt_r.at[c], section=ring(other))

    def add_own(b, c):
        mine = res[lax.rem(b, 2), xh, c]

        @pl.when(b == 2)
        def _():
            rs_out[b, xh, c] = mine.astype(BF16)

        @pl.when(b > 2)
        def _():
            rs_wait(b, xh, c)
            rs_out[b, xh, c] = (mine + rs_in[b, xh, c].astype(F32)).astype(BF16)

        rs_copy(b, xh, c).start()

    def add_other(b, c):
        @pl.when(b < n_y)
        def _():
            mine = res[lax.rem(b, 2), other, c]

            @pl.when(b == 2)
            def _():
                rs_out[b, other, c] = mine.astype(BF16)

            @pl.when(b > 2)
            def _():
                rs_wait(b, other, c)
                rs_out[b, other, c] = (mine + rs_in[b, other, c].astype(F32)).astype(BF16)

            rs_copy(b, other, c).start()

        @pl.when(b == n_y)
        def _():
            rs_wait(n_y, other, c)
            xr_out[c] = (own[other, c] + rs_in[n_y, other, c].astype(F32)).astype(BF16)
            xr_copy(c).start()

    def add_on(t, c):
        @pl.when((t > 3) & (t < n_y + 3))
        def _():
            add_other(t - 2, c)

        @pl.when((t > 4) & (t < n_y + 3))
        def _():
            add_own(t - 3, c)

        @pl.when(t == 4)
        def _():
            rs_cross(c).wait_recv()
            straight_out[c] = (res[1, xh, c] + cross_in[c].astype(F32)).astype(BF16)

        @pl.when(t == n_y + 2)
        def _():
            straight_copy(c).start()

    def down_step(t):
        @pl.when((t > 1) & (t < n_y + 2))
        def _():
            down_product(t - 2)

        @pl.when((t > 4 + RING) & (t < n_y + 3))
        def _():
            rs_sent(t - 3 - RING, xh)

        @pl.when((t > 3 + RING) & (t < n_y + 2))
        def _():
            rs_sent(t - 2 - RING, other)

    def step(t, carry):
        @pl.when(t <= n_y)
        def _():
            gate_up(t - 1)

        @pl.when((t > 1) & (t < n_y - 3))
        def _():
            ag_sent(t - 2, xh)

        @pl.when((t >= RING) & (t < n_y - 2))
        def _():
            ag_sent(t - RING, other)

        for j in range(n_c):
            c = near_first[j]

            @pl.when(t < n_y - 1)
            def _():
                ag_wait(t, other, c)

                @pl.when(t < n_y - 2)
                def _():
                    ag_copy(t, other, c).start()

            @pl.when(t < n_y - 2)
            def _():
                ag_wait(t + 1, xh, c)

                @pl.when(t < n_y - 3)
                def _():
                    ag_copy(t + 1, xh, c).start()

            if j == n_c - 1:

                @pl.when(t == 1)
                def _():
                    ag_last(dr_s, dr_r, section=ring(other)).wait_recv()
                    ag_last(ax_s, ax_r, section=across).start()

            if j == min(PAIR_AT, n_c - 1):

                @pl.when(t <= n_y)
                def _():
                    chip_sum(t - 1)

            if j == min(HIDDEN_AT, n_c - 1):

                @pl.when((t > 1) & (t < n_y + 2))
                def _():
                    hidden_units(t - 2)

            if j == down_at:
                down_step(t - down_late)

            if j >= down_at:
                add_on(t - down_late, far_first[j - down_at])
            else:
                add_on(t - down_late - 1, far_first[j - down_at + n_c])

        return carry

    down_late, down_at = divmod(DOWN_AT * n_c // CHUNKS, n_c)
    lax.fori_loop(1, n_y + 3 + down_late + (down_at > 0), step, 0)

    for c in far_first:
        xr_copy(c).wait_recv()
        answer = own[xh, c] + xr_in[c].astype(F32)
        rs_wait(n_y, xh, c)
        answer = answer + rs_in[n_y, xh, c].astype(F32)
        straight_copy(c).wait_recv()
        answer = answer + straight_in[c].astype(F32)
        for k in range(per):
            zp = c * per + k
            top, below = pack(answer[:, k * n_feat : (k + 1) * n_feat])
            bk_out[zp, 0:cap, :] = top.astype(BF16)
            bk_out[zp, cap : cap + low, :] = jnp.concatenate([below, jnp.zeros((8, LANES), F32)], axis=0).astype(BF16)

            @pl.when(zp != z)
            def _():
                z_copy(bk_out, bk_in, bk_s, bk_r, zp).start()

    bk_in[z] = bk_out[z]

    def z_all(src, send, recv):
        some = src.at[pl.ds(0, n_e - 1)]
        return remote(some, some, send, recv, expert=lax.rem(z + 1, n_e))

    z_all(bk_in, bk_s, bk_r).wait_recv()
    back_top = bk_in[:, 0:cap, :].reshape(n_e * cap, LANES)
    back_low = bk_in[:, cap : cap + low, :].reshape(n_e * low, LANES)
    out_ref[0:LANES, :] = (
        tok_ref[0:LANES, :].astype(F32) + dot_first(back_top, mix_top[0]) + dot_first(back_top, mix_top[1])
    ).astype(BF16)
    low_a = dot_first(back_low, mix_low[0]) + dot_first(back_low, mix_low[1])
    low_b = dot_first(back_low, mix_low[2]) + dot_first(back_low, mix_low[3])
    out_ref[LANES:n_feat, :] = (
        tok_ref[LANES:n_feat, :].astype(F32) + low_a[0:edge] + low_b[edge : 2 * edge]
    ).astype(BF16)

    z_all(go, go_s, go_r.at[0]).wait_send()
    z_all(bk_out, bk_s, bk_r).wait_send()
    d_all(ss_in, ss_s, ss_r).wait_send()
    sx_copy.wait_send()
    remote(ag.at[0, xh], ag.at[0, xh], x_s, x_r.at[0], section=across).wait_send()
    remote(xr_out, xr_out, xr_s, xr_r.at[0], section=across).wait_send()
    for h in range(N_X):
        for b in range(max(0, n_y - 3), n_y - 1):
            sc_copy(b, h).wait_send()
    for b in range(max(0, n_y - 2 - RING), n_y - 2):
        ag_sent(b, xh)
        ag_sent(b, other)
    for b in range(max(2, n_y - RING), n_y):
        rs_sent(b, xh)
        rs_sent(b, other)
    ag_last(dr_s, dr_r, section=ring(other)).wait_send()
    ag_last(ax_s, ax_r, section=across).wait_send()
    remote(straight_out, straight_out, dt_s, dt_r.at[0], section=ring(other)).wait_send()
    remote(cross_out, cross_out, rx_s, rx_r.at[0], section=across).wait_send()
    for b in range(n_y - 2, n_y):
        core_copy(b).wait_send()
    for b in range(max(0, n_y - TURN), n_y):
        pair_copy(b).wait_send()
        hid_copy(b, core).wait_send()


def local(tokens, norm_gain, routes, gates, w_gate, w_up, w_down):
    n_tok, n_feat = tokens.shape
    n_e = lax.axis_size("expert")
    n_d = lax.axis_size("dp")
    n_y = lax.axis_size("section") // N_X
    n_c = min(CHUNKS, n_e)
    cap = min(n_tok, max(2, 3 * n_tok // n_e))
    low = cap // 2 + 8
    width = n_feat * n_e
    wide = width // n_c
    units = w_gate.shape[2]
    unit = units // 2
    rows = N_X * cap
    dma = pltpu.SemaphoreType.DMA
    far = pl.BlockSpec(memory_space=pl.ANY)
    scratch = [
        pltpu.VMEM((n_feat, n_tok), BF16),
        pltpu.VMEM((1, n_feat), F32),
        pltpu.VMEM((2, n_tok), jnp.int32),
        pltpu.VMEM((2, n_tok), F32),
        pltpu.VMEM((width, units), BF16),
        pltpu.VMEM((width, units), BF16),
        pltpu.VMEM((units, width), BF16),
        dma((7,)),
        pltpu.VMEM((2, n_e * cap, n_tok), BF16),
        pltpu.VMEM((4, n_e * low, n_tok), BF16),
        pltpu.VMEM((n_e, cap + low, LANES), BF16),
        pltpu.VMEM((n_e, cap + low, LANES), BF16),
        pltpu.VMEM((8, LANES), F32),
        pltpu.VMEM((n_d - 1, 8, LANES), F32),
        pltpu.VMEM((n_y, N_X, 8, LANES), F32),
        pltpu.VMEM((n_y, N_X, n_c, cap, wide), BF16),
        pltpu.VMEM((n_y, 2, rows, 2 * unit), BF16),
        pltpu.VMEM((n_y, rows, 2 * unit), BF16),
        pltpu.VMEM((n_y, rows, 2 * unit), BF16),
        pltpu.VMEM((n_y, rows, 2 * unit), BF16),
        pltpu.VMEM((n_y, 2, rows, unit), BF16),
        pltpu.VMEM((N_X, n_c, cap, wide), F32),
        pltpu.VMEM((2, N_X, n_c, cap, wide), F32),
        pltpu.VMEM((n_c, cap, wide), BF16),
        pltpu.VMEM((n_c, cap, wide), BF16),
        pltpu.VMEM((n_c, cap, wide), BF16),
        pltpu.VMEM((n_c, cap, wide), BF16),
        pltpu.VMEM((n_y, N_X, n_c, cap, wide), BF16),
        pltpu.VMEM((n_y + 1, N_X, n_c, cap, wide), BF16),
        pltpu.VMEM((n_c, cap, wide), BF16),
        pltpu.VMEM((n_c, cap, wide), BF16),
        pltpu.VMEM((n_e, cap + low, LANES), BF16),
        pltpu.VMEM((n_e, cap + low, LANES), BF16),
        dma,
        dma((n_e,)),
        dma,
        dma,
        dma,
        dma,
        dma((2, N_X)),
        dma((2, N_X)),
        dma,
        dma((n_c,)),
        dma((RING, N_X)),
        dma((RING, N_X, n_c)),
        dma,
        dma,
        dma,
        dma,
        dma((2,)),
        dma((2,)),
        dma((TURN,)),
        dma((TURN,)),
        dma((TURN,)),
        dma((TURN,)),
        dma((RING, N_X)),
        dma((RING, N_X, n_c)),
        dma,
        dma((n_c,)),
        dma,
        dma((n_c,)),
        dma,
        dma((n_c,)),
        dma,
        dma,
    ]
    mixed = pl.pallas_call(
        functools.partial(kernel, (n_y, n_e, n_d, cap, n_c)),
        out_shape=jax.ShapeDtypeStruct((n_feat, n_tok), BF16),
        in_specs=[far] * 7,
        out_specs=pl.BlockSpec(memory_space=pltpu.VMEM),
        scratch_shapes=scratch,
        compiler_params=pltpu.CompilerParams(
            collective_id=0, has_side_effects=True, vmem_limit_bytes=64 * 1024 * 1024
        ),
        name="moe_layer",
    )(tokens.T, norm_gain.reshape(1, n_feat), routes.T, gates.T, w_gate, w_up, w_down)
    return mixed.T


def solution(mesh):
    in_specs = (
        P("section", ("dp", "expert")),
        P(("dp", "expert")),
        P("section", None),
        P("section", None),
        P("expert", "dp", "section"),
        P("expert", "dp", "section"),
        P("expert", "section", "dp"),
    )
    out_specs = P("section", ("dp", "expert"))
    return jax.shard_map(local, mesh=mesh, in_specs=in_specs, out_specs=out_specs, check_vma=False)
```

```python
import functools

import jax
import jax.numpy as jnp
from jax import lax
from jax.experimental import pallas as pl
from jax.experimental.pallas import tpu as pltpu
from jax.sharding import PartitionSpec as P

D = 6144
EPS = 1e-05
N_X = 2
F32 = jnp.float32
BF16 = jnp.bfloat16
LANES = 128
CHUNKS = 4
RING = 3
TURN = 4
PAIR_AT, HIDDEN_AT, DOWN_AT = 1, 3, 4


def dot(a, b):
    return jnp.dot(a, b, preferred_element_type=F32)


def dot_last(a, b):
    return lax.dot_general(a, b, (((1,), (1,)), ((), ())), preferred_element_type=F32)


def dot_first(a, b):
    return lax.dot_general(a, b, (((0,), (0,)), ((), ())), preferred_element_type=F32)


def split3(v):
    high = v.astype(BF16).astype(F32)
    rest = v - high
    mid = rest.astype(BF16).astype(F32)
    return high, mid, rest - mid


def pack(rows):
    half = rows.shape[0] // 2
    tail = rows[:, LANES:]
    return rows[:, :LANES], jnp.concatenate([tail[:half], tail[half:]], axis=1)


def kernel(
    sizes,
    tok_hbm,
    gain_hbm,
    routes_hbm,
    gates_hbm,
    wg_hbm,
    wu_hbm,
    wd_hbm,
    out_ref,
    tok_ref,
    gain_ref,
    routes_ref,
    gates_ref,
    wg,
    wu,
    wd,
    w_sem,
    mix_top,
    mix_low,
    go,
    got,
    ss_out,
    ss_in,
    sc,
    ag,
    part_out,
    core_in,
    pair_out,
    pair_in,
    hid,
    own,
    res,
    cross_out,
    cross_in,
    straight_out,
    straight_in,
    rs_out,
    rs_in,
    xr_out,
    xr_in,
    bk_out,
    bk_in,
    go_s,
    go_r,
    ss_s,
    ss_r,
    sx_s,
    sx_r,
    sc_s,
    sc_r,
    x_s,
    x_r,
    ag_s,
    ag_r,
    dr_s,
    dr_r,
    ax_s,
    ax_r,
    core_s,
    core_r,
    pair_s,
    pair_r,
    hid_s,
    hid_r,
    rs_s,
    rs_r,
    rx_s,
    rx_r,
    dt_s,
    dt_r,
    xr_s,
    xr_r,
    bk_s,
    bk_r,
):
    n_y, n_e, n_d, cap, n_c = sizes
    half = cap // 2
    low = half + 8
    n_feat, n_tok = tok_ref.shape
    edge = n_feat - LANES
    width = n_feat * n_e
    wide = width // n_c
    per = n_e // n_c
    rows = N_X * cap
    sec = lax.axis_index("section")
    z = lax.axis_index("expert")
    d = lax.axis_index("dp")
    xh = lax.div(sec, n_y)
    y = lax.rem(sec, n_y)
    up = xh * n_y + lax.rem(y + 1, n_y)
    down = xh * n_y + lax.rem(y + n_y - 1, n_y)
    across = (1 - xh) * n_y + y
    other = 1 - xh
    chip = lax.div(d, 2)
    core = lax.rem(d, 2)
    mine = lax.div(z, per)
    spread = sorted(range(n_c), key=lambda i: min(i, n_c - i))
    near_first = [lax.rem(mine + i, n_c) for i in spread]
    far_first = near_first[::-1]

    def ring(h):
        return xh * n_y + lax.rem(y + 1 + h * (n_y - 2), n_y)

    def remote(src, dst, send, recv, **where):
        return pltpu.make_async_remote_copy(
            src_ref=src,
            dst_ref=dst,
            send_sem=send,
            recv_sem=recv,
            device_id=where,
            device_id_type=pl.DeviceIdType.MESH,
        )

    barrier = pltpu.get_barrier_semaphore()

    def greet(**where):
        pl.semaphore_signal(barrier, inc=1, device_id=where, device_id_type=pl.DeviceIdType.MESH)

    order = sorted(range(1, n_e), key=lambda i: -min(i, n_e - i))
    for i in order:
        greet(expert=lax.rem(z + i, n_e))
    for to in (across, up, down):
        greet(section=to)
    for i in range(1, n_d):
        greet(dp=lax.rem(d + i, n_d))

    small = [
        pltpu.make_async_copy(src, dst, w_sem.at[i])
        for i, (src, dst) in enumerate(
            ((routes_hbm, routes_ref), (gates_hbm, gates_ref), (tok_hbm, tok_ref), (gain_hbm, gain_ref))
        )
    ]
    loads = [
        pltpu.make_async_copy(src.at[0], dst, w_sem.at[4 + i])
        for i, (src, dst) in enumerate(((wg_hbm, wg), (wu_hbm, wu), (wd_hbm, wd)))
    ]
    for load in small + loads:
        load.start()
    for load in small:
        load.wait()

    first = routes_ref[0:1, :]
    second = routes_ref[1:2, :]
    expert_ids = lax.broadcasted_iota(jnp.int32, (n_e, n_tok), 0)
    named = (first == expert_ids) | (second == expert_ids)
    earlier = (
        lax.broadcasted_iota(jnp.int32, (n_tok, n_tok), 0) < lax.broadcasted_iota(jnp.int32, (n_tok, n_tok), 1)
    )
    count = dot(jnp.where(named, 1.0, 0.0).astype(BF16), jnp.where(earlier, 1.0, 0.0).astype(BF16))
    slot = jnp.where(named, count, -1.0)
    weight = jnp.where(first == expert_ids, gates_ref[0:1, :], gates_ref[1:2, :])
    number = lax.broadcasted_iota(jnp.int32, (cap, n_tok), 0).astype(F32)
    picks = [jnp.where(slot[e : e + 1, :] == number, 1.0, 0.0) for e in range(n_e)]
    eye = lax.broadcasted_iota(jnp.int32, (cap, LANES), 0) == lax.broadcasted_iota(jnp.int32, (cap, LANES), 1)
    picked = dot_last(jnp.concatenate([p.astype(BF16) for p in picks], axis=0), tok_ref[...])
    squares = jnp.sum(picked * picked, axis=1, keepdims=True)
    picked = picked * gain_ref[...]
    for e in range(n_e):
        top, below = pack(picked[e * cap : (e + 1) * cap])
        go[e, 0:cap, :] = top.astype(BF16)
        terms = split3(jnp.sum(jnp.where(eye, squares[e * cap : (e + 1) * cap], 0.0), axis=0, keepdims=True))
        go[e, cap : cap + low, :] = jnp.concatenate(
            [below] + list(terms) + [jnp.zeros((5, LANES), F32)], axis=0
        ).astype(BF16)

    pl.semaphore_wait(barrier, n_e - 1 + n_d - 1 + 3)

    def z_copy(src, dst, send, recv, to):
        return remote(src.at[to], dst.at[z], send, recv, expert=to)

    for i in order[::-1]:
        z_copy(go, got, go_s, go_r.at[z], lax.rem(z + i, n_e)).start()
    got[z] = go[z]

    def x_copy(c):
        return remote(ag.at[0, xh, c], ag.at[0, xh, c], x_s, x_r.at[c], section=across)

    def ag_copy(b, h, c):
        at = lax.rem(b, RING)
        return remote(
            ag.at[b, h, c], ag.at[b + 1, h, c], ag_s.at[at, h], ag_r.at[lax.rem(b + 1, RING), h, c], section=ring(h)
        )

    def ag_sent(b, h):
        remote(ag.at[b, h], ag.at[b, h], ag_s.at[lax.rem(b, RING), h], ag_r.at[0, h, 0], section=ring(h)).wait_send()

    def ag_wait(b, h, c):
        at = lax.rem(b, RING)
        remote(ag.at[b, h, c], ag.at[b, h, c], ag_s.at[at, h], ag_r.at[at, h, c], section=ring(h)).wait_recv()

    def ag_straight(c):
        return remote(ag.at[0, xh, c], ag.at[n_y - 1, xh, c], dr_s, dr_r, section=ring(other))

    def ag_last(send, recv, **where):
        return remote(ag.at[n_y - 1, xh], ag.at[n_y - 1, xh], send, recv, **where)

    low_row = lax.broadcasted_iota(jnp.int32, (low, n_tok), 0)
    low_number = jnp.where(low_row < half, low_row, 4 * cap).astype(F32)
    for e in range(n_e):
        mark = slot[e : e + 1, :]
        w = weight[e : e + 1, :]
        for part, store, lead, size in (
            (picks[e], mix_top, 0, cap),
            (jnp.where(mark == low_number, 1.0, 0.0), mix_low, 0, low),
            (jnp.where(mark == low_number + half, 1.0, 0.0), mix_low, 2, low),
        ):
            value = part * w
            high = value.astype(BF16)
            store[lead, e * size : (e + 1) * size, :] = high
            store[lead + 1, e * size : (e + 1) * size, :] = (value - high.astype(F32)).astype(BF16)

    row_squares = jnp.zeros((1, LANES), F32)
    for c in near_first:
        pieces = []
        for k in range(per):
            zp = c * per + k

            @pl.when(zp != z)
            def _():
                remote(go.at[zp], got.at[zp], go_s, go_r.at[zp], expert=zp).wait_recv()

            block = got[zp].astype(F32)
            below = block[cap : cap + half]
            pieces.append(
                jnp.concatenate(
                    [block[:cap], jnp.concatenate([below[:, :edge], below[:, edge : 2 * edge]], axis=0)], axis=1
                )
            )
            terms = block[cap + half : cap + half + 8]
            row_squares = row_squares + (terms[0:1] + terms[1:2] + terms[2:3])
        ag[0, xh, c] = jnp.concatenate(pieces, axis=1).astype(BF16)
        x_copy(c).start()
        ag_straight(c).start()
        ag_copy(0, xh, c).start()

    def d_copy(src, dst, send, recv, i):
        return remote(src, dst.at[i - 1], send, recv, dp=lax.rem(d + i, n_d))

    def d_all(dst, send, recv):
        return remote(dst, dst, send, recv, dp=lax.rem(d + 1, n_d))

    ss_out[...] = jnp.broadcast_to(row_squares, ss_out.shape)
    for i in range(1, n_d):
        d_copy(ss_out, ss_in, ss_s, ss_r, i).start()
    for c in near_first:
        ag_wait(1, xh, c)
        ag_copy(1, xh, c).start()
        remote(ag.at[0, other, c], ag.at[0, other, c], x_s, x_r.at[c], section=across).wait_recv()
        ag_copy(0, other, c).start()
    d_all(ss_in, ss_s, ss_r).wait_recv()
    total = row_squares
    for i in range(n_d - 1):
        total = total + ss_in[i][0:1, :]
    sc[0, xh] = jnp.broadcast_to(lax.rsqrt(total / (n_d * width) + EPS), ss_out.shape)
    sx_copy = remote(sc.at[0, xh], sc.at[0, xh], sx_s, sx_r, section=across)
    sx_copy.start()
    for load in loads:
        load.wait()

    def sc_copy(b, h):
        at = lax.rem(b, 2)
        return remote(sc.at[b, h], sc.at[b + 1, h], sc_s.at[at, h], sc_r.at[1 - at, h], section=ring(h))

    def core_copy(b):
        at = lax.rem(b, 2)
        return remote(part_out.at[b, 1 - core], core_in.at[b], core_s.at[at], core_r.at[at], dp=2 * chip + 1 - core)

    def pair_copy(b):
        at = lax.rem(b, TURN)
        return remote(pair_out.at[b], pair_in.at[b], pair_s.at[at], pair_r.at[at], dp=2 * (1 - chip) + core)

    def hid_copy(b, which):
        at = lax.rem(b, TURN)
        return remote(hid.at[b, which], hid.at[b, which], hid_s.at[at], hid_r.at[at], dp=2 * chip + 1 - core)

    def rs_copy(b, h, c):
        return remote(
            rs_out.at[b, h, c],
            rs_in.at[b + 1, h, c],
            rs_s.at[lax.rem(b, RING), h],
            rs_r.at[lax.rem(b + 1, RING), h, c],
            section=ring(h),
        )

    def rs_wait(b, h, c):
        at = lax.rem(b, RING)
        remote(rs_in.at[b, h, c], rs_in.at[b, h, c], rs_s.at[at, h], rs_r.at[at, h, c], section=ring(h)).wait_recv()

    def rs_sent(b, h):
        some = rs_out.at[b, h]
        remote(some, some, rs_s.at[lax.rem(b, RING), h], rs_r.at[0, h, 0], section=ring(h)).wait_send()

    unit = wg.shape[1] // 2

    def gate_up(b):
        @pl.when(b > 1)
        def _():
            core_copy(b - 2).wait_send()

        @pl.when(b == n_y - 1)
        def _():
            last = ag.at[n_y - 1, other]
            remote(last, last, ax_s, ax_r, section=across).wait_recv()

        block = jnp.concatenate([ag[b, :, c].reshape(rows, wide) for c in range(n_c)], axis=1)
        gate = dot(block, wg[...]).astype(BF16)
        upper = dot(block, wu[...]).astype(BF16)
        for p in range(2):
            part_out[b, p, :, 0:unit] = gate[:, p * unit : (p + 1) * unit]
            part_out[b, p, :, unit : 2 * unit] = upper[:, p * unit : (p + 1) * unit]
        core_copy(b).start()

    def chip_sum(b):
        @pl.when(b >= TURN)
        def _():
            pair_copy(b - TURN).wait_send()

        core_copy(b).wait_recv()
        pair_out[b] = (part_out[b, core].astype(F32) + core_in[b].astype(F32)).astype(BF16)
        pair_copy(b).start()

    def hidden_units(b):
        @pl.when(b == 0)
        def _():
            remote(sc.at[0, 1 - xh], sc.at[0, 1 - xh], sx_s, sx_r, section=across).wait_recv()

        @pl.when(b > 0)
        def _():
            for h in range(N_X):
                remote(
                    sc.at[b, h], sc.at[b, h], sc_s.at[0, h], sc_r.at[lax.rem(b, 2), h], section=ring(h)
                ).wait_recv()

        @pl.when((b > 1) & (b < n_y - 1))
        def _():
            for h in range(N_X):
                sc_copy(b - 2, h).wait_send()

        @pl.when(b < n_y - 1)
        def _():
            for h in range(N_X):
                sc_copy(b, h).start()

        @pl.when(b >= TURN)
        def _():
            hid_copy(b - TURN, core).wait_send()

        scales = [jnp.sum(jnp.where(eye, sc[b, h][0:1, :], 0.0), axis=1, keepdims=True) for h in range(N_X)]
        pair_copy(b).wait_recv()
        both = part_out[b, core].astype(F32) + core_in[b].astype(F32) + pair_in[b].astype(F32)
        both = both * jnp.concatenate(scales, axis=0)
        g = both[:, 0:unit]
        hid[b, core] = (g / (1.0 + jnp.exp(-g)) * both[:, unit : 2 * unit]).astype(BF16)
        hid_copy(b, core).start()

    def down_product(b):
        hid_copy(b, 1 - core).wait_recv()
        result = dot(jnp.concatenate([hid[b, 0], hid[b, 1]], axis=1), wd[...])

        def keep(ref):
            for h in range(N_X):
                for c in range(n_c):
                    ref[h, c] = result[h * cap : (h + 1) * cap, c * wide : (c + 1) * wide]

        @pl.when(b == 0)
        def _():
            keep(own)

        @pl.when(b > 0)
        def _():
            keep(res.at[lax.rem(b, 2)])

        @pl.when(b == 1)
        def _():
            for c in far_first:
                cross_out[c] = res[1, other, c].astype(BF16)
                rs_cross(c).start()

    def rs_cross(c):
        return remote(cross_out.at[c], cross_in.at[c], rx_s, rx_r.at[c], section=across)

    def xr_copy(c):
        return remote(xr_out.at[c], xr_in.at[c], xr_s, xr_r.at[c], section=across)

    def straight_copy(c):
        return remote(straight_out.at[c], straight_in.at[c], dt_s, dt_r.at[c], section=ring(other))

    def add_own(b, c):
        mine = res[lax.rem(b, 2), xh, c]

        @pl.when(b == 2)
        def _():
            rs_out[b, xh, c] = mine.astype(BF16)

        @pl.when(b > 2)
        def _():
            rs_wait(b, xh, c)
            rs_out[b, xh, c] = (mine + rs_in[b, xh, c].astype(F32)).astype(BF16)

        rs_copy(b, xh, c).start()

    def add_other(b, c):
        @pl.when(b < n_y)
        def _():
            mine = res[lax.rem(b, 2), other, c]

            @pl.when(b == 2)
            def _():
                rs_out[b, other, c] = mine.astype(BF16)

            @pl.when(b > 2)
            def _():
                rs_wait(b, other, c)
                rs_out[b, other, c] = (mine + rs_in[b, other, c].astype(F32)).astype(BF16)

            rs_copy(b, other, c).start()

        @pl.when(b == n_y)
        def _():
            rs_wait(n_y, other, c)
            xr_out[c] = (own[other, c] + rs_in[n_y, other, c].astype(F32)).astype(BF16)
            xr_copy(c).start()

    def add_on(t, c):
        @pl.when((t > 3) & (t < n_y + 3))
        def _():
            add_other(t - 2, c)

        @pl.when((t > 4) & (t < n_y + 3))
        def _():
            add_own(t - 3, c)

        @pl.when(t == 4)
        def _():
            rs_cross(c).wait_recv()
            straight_out[c] = (res[1, xh, c] + cross_in[c].astype(F32)).astype(BF16)

        @pl.when(t == n_y + 2)
        def _():
            straight_copy(c).start()

    def down_step(t):
        @pl.when((t > 1) & (t < n_y + 2))
        def _():
            down_product(t - 2)

        @pl.when((t > 4 + RING) & (t < n_y + 3))
        def _():
            rs_sent(t - 3 - RING, xh)

        @pl.when((t > 3 + RING) & (t < n_y + 2))
        def _():
            rs_sent(t - 2 - RING, other)

    def step(t, carry):
        @pl.when((t > 1) & (t < n_y - 3))
        def _():
            ag_sent(t - 2, xh)

        @pl.when((t >= RING) & (t < n_y - 2))
        def _():
            ag_sent(t - RING, other)

        for j in range(n_c):
            c = near_first[j]

            @pl.when(t < n_y - 1)
            def _():
                ag_wait(t, other, c)

                @pl.when(t < n_y - 2)
                def _():
                    ag_copy(t, other, c).start()

            @pl.when(t < n_y - 2)
            def _():
                ag_wait(t + 1, xh, c)

                @pl.when(t < n_y - 3)
                def _():
                    ag_copy(t + 1, xh, c).start()

            if j == n_c - 1:

                @pl.when(t == 1)
                def _():
                    ag_last(dr_s, dr_r, section=ring(other)).wait_recv()
                    ag_last(ax_s, ax_r, section=across).start()

            if j == 0:

                @pl.when(t <= n_y)
                def _():
                    gate_up(t - 1)

            if j == min(PAIR_AT, n_c - 1):

                @pl.when(t <= n_y)
                def _():
                    chip_sum(t - 1)

            if j == min(HIDDEN_AT, n_c - 1):

                @pl.when((t > 1) & (t < n_y + 2))
                def _():
                    hidden_units(t - 2)

            if j == down_at:
                down_step(t - down_late)

            if j >= down_at:
                add_on(t - down_late, far_first[j - down_at])
            else:
                add_on(t - down_late - 1, far_first[j - down_at + n_c])

        return carry

    down_late, down_at = divmod(DOWN_AT * n_c // CHUNKS, n_c)
    lax.fori_loop(1, n_y + 3 + down_late + (down_at > 0), step, 0)

    for c in far_first:
        xr_copy(c).wait_recv()
        answer = own[xh, c] + xr_in[c].astype(F32)
        rs_wait(n_y, xh, c)
        answer = answer + rs_in[n_y, xh, c].astype(F32)
        straight_copy(c).wait_recv()
        answer = answer + straight_in[c].astype(F32)
        for k in range(per):
            zp = c * per + k
            top, below = pack(answer[:, k * n_feat : (k + 1) * n_feat])
            bk_out[zp, 0:cap, :] = top.astype(BF16)
            bk_out[zp, cap : cap + low, :] = jnp.concatenate([below, jnp.zeros((8, LANES), F32)], axis=0).astype(BF16)

            @pl.when(zp != z)
            def _():
                z_copy(bk_out, bk_in, bk_s, bk_r, zp).start()

    bk_in[z] = bk_out[z]

    def z_all(src, send, recv):
        some = src.at[pl.ds(0, n_e - 1)]
        return remote(some, some, send, recv, expert=lax.rem(z + 1, n_e))

    z_all(bk_in, bk_s, bk_r).wait_recv()
    back_top = bk_in[:, 0:cap, :].reshape(n_e * cap, LANES)
    back_low = bk_in[:, cap : cap + low, :].reshape(n_e * low, LANES)
    out_ref[0:LANES, :] = (
        tok_ref[0:LANES, :].astype(F32) + dot_first(back_top, mix_top[0]) + dot_first(back_top, mix_top[1])
    ).astype(BF16)
    low_a = dot_first(back_low, mix_low[0]) + dot_first(back_low, mix_low[1])
    low_b = dot_first(back_low, mix_low[2]) + dot_first(back_low, mix_low[3])
    out_ref[LANES:n_feat, :] = (
        tok_ref[LANES:n_feat, :].astype(F32) + low_a[0:edge] + low_b[edge : 2 * edge]
    ).astype(BF16)

    z_all(go, go_s, go_r.at[0]).wait_send()
    z_all(bk_out, bk_s, bk_r).wait_send()
    d_all(ss_in, ss_s, ss_r).wait_send()
    sx_copy.wait_send()
    remote(ag.at[0, xh], ag.at[0, xh], x_s, x_r.at[0], section=across).wait_send()
    remote(xr_out, xr_out, xr_s, xr_r.at[0], section=across).wait_send()
    for h in range(N_X):
        for b in range(max(0, n_y - 3), n_y - 1):
            sc_copy(b, h).wait_send()
    for b in range(max(0, n_y - 2 - RING), n_y - 2):
        ag_sent(b, xh)
        ag_sent(b, other)
    for b in range(max(2, n_y - RING), n_y):
        rs_sent(b, xh)
        rs_sent(b, other)
    ag_last(dr_s, dr_r, section=ring(other)).wait_send()
    ag_last(ax_s, ax_r, section=across).wait_send()
    remote(straight_out, straight_out, dt_s, dt_r.at[0], section=ring(other)).wait_send()
    remote(cross_out, cross_out, rx_s, rx_r.at[0], section=across).wait_send()
    for b in range(n_y - 2, n_y):
        core_copy(b).wait_send()
    for b in range(max(0, n_y - TURN), n_y):
        pair_copy(b).wait_send()
        hid_copy(b, core).wait_send()


def local(tokens, norm_gain, routes, gates, w_gate, w_up, w_down):
    n_tok, n_feat = tokens.shape
    n_e = lax.axis_size("expert")
    n_d = lax.axis_size("dp")
    n_y = lax.axis_size("section") // N_X
    n_c = min(CHUNKS, n_e)
    cap = min(n_tok, max(2, 3 * n_tok // n_e))
    low = cap // 2 + 8
    width = n_feat * n_e
    wide = width // n_c
    units = w_gate.shape[2]
    unit = units // 2
    rows = N_X * cap
    dma = pltpu.SemaphoreType.DMA
    far = pl.BlockSpec(memory_space=pl.ANY)
    scratch = [
        pltpu.VMEM((n_feat, n_tok), BF16),
        pltpu.VMEM((1, n_feat), F32),
        pltpu.VMEM((2, n_tok), jnp.int32),
        pltpu.VMEM((2, n_tok), F32),
        pltpu.VMEM((width, units), BF16),
        pltpu.VMEM((width, units), BF16),
        pltpu.VMEM((units, width), BF16),
        dma((7,)),
        pltpu.VMEM((2, n_e * cap, n_tok), BF16),
        pltpu.VMEM((4, n_e * low, n_tok), BF16),
        pltpu.VMEM((n_e, cap + low, LANES), BF16),
        pltpu.VMEM((n_e, cap + low, LANES), BF16),
        pltpu.VMEM((8, LANES), F32),
        pltpu.VMEM((n_d - 1, 8, LANES), F32),
        pltpu.VMEM((n_y, N_X, 8, LANES), F32),
        pltpu.VMEM((n_y, N_X, n_c, cap, wide), BF16),
        pltpu.VMEM((n_y, 2, rows, 2 * unit), BF16),
        pltpu.VMEM((n_y, rows, 2 * unit), BF16),
        pltpu.VMEM((n_y, rows, 2 * unit), BF16),
        pltpu.VMEM((n_y, rows, 2 * unit), BF16),
        pltpu.VMEM((n_y, 2, rows, unit), BF16),
        pltpu.VMEM((N_X, n_c, cap, wide), F32),
        pltpu.VMEM((2, N_X, n_c, cap, wide), F32),
        pltpu.VMEM((n_c, cap, wide), BF16),
        pltpu.VMEM((n_c, cap, wide), BF16),
        pltpu.VMEM((n_c, cap, wide), BF16),
        pltpu.VMEM((n_c, cap, wide), BF16),
        pltpu.VMEM((n_y, N_X, n_c, cap, wide), BF16),
        pltpu.VMEM((n_y + 1, N_X, n_c, cap, wide), BF16),
        pltpu.VMEM((n_c, cap, wide), BF16),
        pltpu.VMEM((n_c, cap, wide), BF16),
        pltpu.VMEM((n_e, cap + low, LANES), BF16),
        pltpu.VMEM((n_e, cap + low, LANES), BF16),
        dma,
        dma((n_e,)),
        dma,
        dma,
        dma,
        dma,
        dma((2, N_X)),
        dma((2, N_X)),
        dma,
        dma((n_c,)),
        dma((RING, N_X)),
        dma((RING, N_X, n_c)),
        dma,
        dma,
        dma,
        dma,
        dma((2,)),
        dma((2,)),
        dma((TURN,)),
        dma((TURN,)),
        dma((TURN,)),
        dma((TURN,)),
        dma((RING, N_X)),
        dma((RING, N_X, n_c)),
        dma,
        dma((n_c,)),
        dma,
        dma((n_c,)),
        dma,
        dma((n_c,)),
        dma,
        dma,
    ]
    mixed = pl.pallas_call(
        functools.partial(kernel, (n_y, n_e, n_d, cap, n_c)),
        out_shape=jax.ShapeDtypeStruct((n_feat, n_tok), BF16),
        in_specs=[far] * 7,
        out_specs=pl.BlockSpec(memory_space=pltpu.VMEM),
        scratch_shapes=scratch,
        compiler_params=pltpu.CompilerParams(
            collective_id=0, has_side_effects=True, vmem_limit_bytes=64 * 1024 * 1024
        ),
        name="moe_layer",
    )(tokens.T, norm_gain.reshape(1, n_feat), routes.T, gates.T, w_gate, w_up, w_down)
    return mixed.T


def solution(mesh):
    in_specs = (
        P("section", ("dp", "expert")),
        P(("dp", "expert")),
        P("section", None),
        P("section", None),
        P("expert", "dp", "section"),
        P("expert", "dp", "section"),
        P("expert", "section", "dp"),
    )
    out_specs = P("section", ("dp", "expert"))
    return jax.shard_map(local, mesh=mesh, in_specs=in_specs, out_specs=out_specs, check_vma=False)
```
